128 devices in a mesh: dp: 16 (over x, y_hi, core), shard: 8 (over y_lo, z).
Axes of the slice: x: 4, y: 4 (y_hi: 2, y_lo: 2; y = y_hi * 2 + y_lo), z: 4, core: 2. Of those that a mesh axis runs over, the one named last changes fastest.
Arguments:
- gradients: bfloat16 [16, 3968, 3968], P('dp', None, 'shard'), may hold values from -12 to 12
- error_memory: float32 [16, 3968, 3968], P('dp', None, 'shard'), may hold values from -9 to 9
- q_factor: bfloat16 [3968, 1024], P('shard'), may hold values from -0.09375 to 0.09375
Outputs:
- rebuilt: bfloat16 [3968, 3968], P(None, 'shard')
- new_error: float32 [16, 3968, 3968], P('dp', None, 'shard')
The draws below stay inside these ranges and needn't reach their ends.
All inputs are finite; a program needn't handle non-finite values.
Results may differ from the reference program's by a relative error of at most 0.0072.
Values may be sent and summed in bfloat16 or wider, within the bound.
No kernel may reach another device: no remote copies, remote signals or barrier semaphores. Data moves between devices by JAX's collectives and lax.ppermute only.
A program may use at most 192 MiB of HBM per device.

```python
import jax
import jax.numpy as jnp
from jax import lax

D = 3968
RANK = 1024
REPLICAS = 16
N_DP = 16


def shard_levels(own_key, shape, pieces, least, largest):
    factor_of = 1.0
    for position, parts in pieces:
        steps = jax.random.uniform(jax.random.fold_in(jax.random.fold_in(own_key, 6), position), (parts,), jnp.float32, least / len(pieces), largest / len(pieces))
        factor_of = factor_of * jnp.repeat(jnp.exp(steps), shape[position] // parts).reshape((-1,) + (1,) * (len(shape) - 1 - position))
    return factor_of


def noise(stream_key, extent, width, most, shards=(), dtype=jnp.bfloat16):
    gain = shard_levels(stream_key, extent, shards, -0.22, 0.18) if shards else 1.0
    array = jax.random.normal(stream_key, extent, jnp.float32) * width * gain
    return jnp.minimum(jnp.maximum(array, -most), most).astype(dtype)


def setup_inputs(seed: int = 0) -> dict:
    key_list = jax.random.split(jax.random.key(seed), 4)
    return {
        "gradients": noise(key_list[0], (REPLICAS, D, D), 2.0, 12.0, ((0, 16), (2, 8))),
        "error_memory": noise(key_list[1], (REPLICAS, D, D), 1.5, 9.0, ((0, 16), (2, 8)), jnp.float32),
        "q_factor": noise(key_list[2], (D, RANK), D ** -0.5, 0.09375, ((0, 8),)),
    }


def reference(gradients, error_memory, q_factor):
    combined_f = gradients.astype(jnp.float32) + error_memory
    combined = lax.optimization_barrier(combined_f.astype(jnp.bfloat16))
    total = jnp.sum(combined.astype(jnp.float32), axis=0)
    p_sum = jnp.dot(total, q_factor.astype(jnp.float32), precision=lax.Precision.HIGHEST)
    gram_matrix = jnp.dot(p_sum.T, p_sum, precision=lax.Precision.HIGHEST)
    cholesky_factor = jnp.linalg.cholesky(gram_matrix)
    basis = lax.linalg.triangular_solve(cholesky_factor, p_sum, left_side=False, lower=True, transpose_a=True)
    basis = lax.optimization_barrier(basis.astype(jnp.bfloat16))
    q_new = jnp.dot(total.T, basis.astype(jnp.float32), precision=lax.Precision.HIGHEST) / N_DP
    q_new = q_new.astype(jnp.bfloat16)
    rebuilt_f = jnp.dot(basis.astype(jnp.float32), q_new.T.astype(jnp.float32), preferred_element_type=jnp.float32)
    new_error = combined_f - rebuilt_f[None]
    return (rebuilt_f.astype(jnp.bfloat16), new_error)
```

```python
import jax
import jax.numpy as jnp
from jax import lax
from jax.sharding import Mesh, PartitionSpec as P

f32 = jnp.float32
bf16 = jnp.bfloat16
HIGHEST = lax.Precision.HIGHEST

CHIPS = ("x", "yh")
CORE = "c"
SHARD = ("yl", "z")
DP = CHIPS + (CORE,)
SWAP = [(0, 1), (1, 0)]


def dot(a, b, dims, precision=HIGHEST):
    return lax.dot_general(a, b, (dims, ((), ())), precision=precision, preferred_element_type=f32)


def spread(a, axes, n):
    blocks = jnp.broadcast_to(a[None], (n,) + a.shape)
    return lax.all_to_all(blocks, axes, 0, 0, tiled=True)


def halves(blocks, core):
    first = core == 0
    return (
        jnp.where(first, blocks[:, 0], blocks[:, 1]),
        jnp.where(first, blocks[:, 1], blocks[:, 0]),
    )


def factor_solve(gram_matrix, rhs):
    factor = jnp.linalg.cholesky(gram_matrix)
    return lax.linalg.triangular_solve(factor, rhs, left_side=True, lower=True)


def shards(gradients, error_memory, q_factor):
    core = lax.axis_index(CORE)
    n_chips = lax.axis_size(CHIPS)
    n_dp = 2 * n_chips
    n_sh = lax.axis_size(SHARD)
    rows, cols = gradients.shape[1:]
    rank = q_factor.shape[1]
    own = rows // n_dp
    wide = -(-cols // 128) * 128

    with jax.named_scope("total"):
        combined_f = gradients[0].astype(f32) + error_memory[0]
        combined = combined_f.astype(bf16)
        mine, other = halves(combined.reshape(n_chips, 2, own, cols), core)
        got = lax.ppermute(other, CORE, SWAP)
        pair = (mine.astype(f32) + got.astype(f32)).astype(bf16)
        arrived = lax.all_to_all(pair, CHIPS, 0, 0, tiled=True)
        total = jnp.sum(arrived.astype(f32), axis=0)

    with jax.named_scope("left"):
        part = dot(q_factor.astype(f32), total, ((0,), (1,)))
        arrived = lax.all_to_all(part.reshape(n_sh, rank // n_sh, own), SHARD, 0, 0, tiled=True)
        p_own = jnp.sum(arrived, axis=0)
        p_t = spread(p_own, SHARD, n_sh).reshape(rank, own)

    with jax.named_scope("gram"):
        gram_part = dot(p_own, p_t, ((1,), (1,)))
        total_wide = jnp.pad(total, ((0, 0), (0, wide - cols)))
        w_part = dot(total_wide, p_t, ((0,), (1,)))
        g_rows = rank // n_sh // n_dp
        w_rows = wide // n_dp
        blocks = jnp.concatenate(
            [gram_part.reshape(n_dp, g_rows, rank), w_part.reshape(n_dp, w_rows, rank)], axis=1
        )
        mine, other = halves(blocks.reshape(n_chips, 2, g_rows + w_rows, rank), core)
        got = lax.ppermute(other, CORE, SWAP)
        arrived = lax.all_to_all(mine + got, CHIPS, 0, 0, tiled=True)
        summed = jnp.sum(arrived, axis=0)
        gram_matrix = spread(summed[:g_rows], SHARD + DP, n_sh * n_dp).reshape(rank, rank)

    with jax.named_scope("solve"):
        solved = factor_solve(gram_matrix, jnp.concatenate([p_t, summed[g_rows:].T], axis=1))
        basis_t = solved[:, :own].astype(bf16)
        q_own = (solved[:, own:].T / n_dp).astype(bf16)

    with jax.named_scope("rebuild"):
        q_new = spread(q_own, DP, n_dp).reshape(wide, rank)
        block = dot(basis_t, q_new[:cols], ((0,), (1,)), None).astype(bf16)
        near = spread(block, CHIPS, n_chips)
        far = lax.ppermute(near, CORE, SWAP)
        first = core == 0
        both = jnp.stack([jnp.where(first, near, far), jnp.where(first, far, near)], axis=1)
        rebuilt = both.reshape(rows, cols)
        combined_f = gradients[0].astype(f32) + error_memory[0]
        new_error = combined_f - rebuilt.astype(f32)
    return (rebuilt, new_error[None])


def solution(mesh):
    fine = Mesh(mesh.devices.reshape(4, 2, 2, 2, 4), ("x", "yh", "c", "yl", "z"))
    in_specs = (P(DP, None, SHARD), P(DP, None, SHARD), P(SHARD, None))
    out_specs = (P(None, SHARD), P(DP, None, SHARD))
    return jax.shard_map(shards, mesh=fine, in_specs=in_specs, out_specs=out_specs, check_vma=False)
```

```python
import functools

import jax
import jax.numpy as jnp
from jax import lax
from jax.experimental import pallas as pl
from jax.experimental.pallas import tpu as pltpu
from jax.sharding import Mesh, PartitionSpec as P

f32 = jnp.float32
bf16 = jnp.bfloat16
HIGHEST = lax.Precision.HIGHEST

CHIPS = ("x", "yh")
CORE = "c"
SHARD = ("yl", "z")
DP = CHIPS + (CORE,)
SWAP = [(0, 1), (1, 0)]

TILE, LANES = 8, 128
VMEM_LIMIT = 48 * 2**20


def dot(a, b, dims, precision=HIGHEST):
    return lax.dot_general(a, b, (dims, ((), ())), precision=precision, preferred_element_type=f32)


def spread(a, axes, n):
    blocks = jnp.broadcast_to(a[None], (n,) + a.shape)
    return lax.all_to_all(blocks, axes, 0, 0, tiled=True)


def halves(blocks, core):
    first = core == 0
    return (
        jnp.where(first, blocks[:, 0], blocks[:, 1]),
        jnp.where(first, blocks[:, 1], blocks[:, 0]),
    )


def cut_kernel(rows, core_ref, g_ref, e_ref, mine_ref, other_ref):
    core = core_ref[0]
    width = mine_ref.shape[2]
    combined = g_ref[...].astype(f32) + e_ref[...]
    at = pl.program_id(0) * 2 * width + lax.broadcasted_iota(jnp.int32, combined.shape, 1)
    combined = jnp.where(at < rows, combined, 0.0).astype(bf16)
    low, high = combined[:, :width], combined[:, width:]

    @pl.when(core == 0)
    def _():
        mine_ref[0], other_ref[0] = low, high

    @pl.when(core != 0)
    def _():
        mine_ref[0], other_ref[0] = high, low


def cut(core, gradient_t, error_t, n_chips, width):
    cols, rows = gradient_t.shape
    whole = pl.BlockSpec((cols, 2 * width), lambda i, core: (0, i))
    part = pl.BlockSpec((1, cols, width), lambda i, core: (i, 0, 0))
    shape = jax.ShapeDtypeStruct((n_chips, cols, width), bf16)
    return pl.pallas_call(
        functools.partial(cut_kernel, rows),
        grid_spec=pltpu.PrefetchScalarGridSpec(
            num_scalar_prefetch=1, grid=(n_chips,), in_specs=[whole, whole], out_specs=[part, part]
        ),
        out_shape=[shape, shape],
        compiler_params=pltpu.CompilerParams(vmem_limit_bytes=VMEM_LIMIT),
        name="cut",
    )(core[None], gradient_t, error_t)


def finish_kernel(core_ref, near_ref, far_ref, g_ref, e_ref, rebuilt_ref, error_ref):
    core = core_ref[0]
    width = near_ref.shape[2]

    def store(columns, block):
        rebuilt_ref[:, columns] = block
        combined = g_ref[:, columns].astype(f32) + e_ref[:, columns]
        error_ref[:, columns] = combined - block.astype(f32)

    low, high = pl.ds(0, width), pl.ds(width, width)

    @pl.when(core == 0)
    def _():
        store(low, near_ref[0])
        store(high, far_ref[0])

    @pl.when(core != 0)
    def _():
        store(low, far_ref[0])
        store(high, near_ref[0])


def finish(core, near, far, gradient_t, error_t):
    cols, rows = gradient_t.shape
    n_chips, _, width = near.shape
    whole = pl.BlockSpec((cols, 2 * width), lambda i, core: (0, i))
    part = pl.BlockSpec((1, cols, width), lambda i, core: (i, 0, 0))
    return pl.pallas_call(
        finish_kernel,
        grid_spec=pltpu.PrefetchScalarGridSpec(
            num_scalar_prefetch=1,
            grid=(n_chips,),
            in_specs=[part, part, whole, whole],
            out_specs=[whole, whole],
        ),
        out_shape=[
            jax.ShapeDtypeStruct((cols, rows), bf16),
            jax.ShapeDtypeStruct((cols, rows), f32),
        ],
        compiler_params=pltpu.CompilerParams(vmem_limit_bytes=VMEM_LIMIT),
        name="finish",
    )(core[None], near, far, gradient_t, error_t)


def inverse_factor(block):
    n = LANES // TILE
    sub = lax.broadcasted_iota(jnp.int32, (TILE, LANES), 0)
    lane = lax.broadcasted_iota(jnp.int32, (TILE, LANES), 1)
    left = [block[TILE * t : TILE * (t + 1)] for t in range(n)]
    right = [jnp.where(lane == sub + TILE * t, 1.0, 0.0).astype(f32) for t in range(n)]
    full = lambda v: jnp.broadcast_to(v, (TILE, LANES))
    out = []
    for t in range(n):
        at = TILE * t
        rows_l = [full(left[t][k : k + 1]) for k in range(TILE)]
        rows_r = [full(right[t][k : k + 1]) for k in range(TILE)]
        cols = [full(left[t][:, at + k : at + k + 1]) for k in range(TILE)]
        s = [[full(cols[k][i : i + 1]) for k in range(i + 1)] for i in range(TILE)]
        later = range(t + 1, n)
        e = {p: [full(left[p][:, at + k : at + k + 1]) for k in range(TILE)] for p in later}
        pivots = result = None
        for k in range(TILE):
            d = s[k][k]
            inv = 1.0 / d
            l = {i: s[i][k] * inv for i in range(k + 1, TILE)}
            for i in range(k + 1, TILE):
                for m in range(k + 1, i + 1):
                    s[i][m] = s[i][m] - l[i] * s[m][k]
            scaled_l, scaled_r = rows_l[k] * inv, rows_r[k] * inv
            for i in range(k + 1, TILE):
                rows_l[i] = rows_l[i] - l[i] * rows_l[k]
                rows_r[i] = rows_r[i] - l[i] * rows_r[k]
            for p in later:
                left[p] = left[p] - e[p][k] * scaled_l
                right[p] = right[p] - e[p][k] * scaled_r
                for i in range(k + 1, TILE):
                    e[p][i] = e[p][i] - l[i] * e[p][k]
            pivots = d if k == 0 else jnp.where(sub == k, d, pivots)
            result = rows_r[k] if k == 0 else jnp.where(sub == k, rows_r[k], result)
        out.append(result * lax.rsqrt(pivots))
    return out


def solve_kernel(core_ref, near_hbm, far_hbm, z_hbm, y_ref, a, linv, u, sems):
    half, rank = near_hbm.shape
    core = core_ref[0]
    own = pl.multiple_of(core * half, half)
    others = pl.multiple_of((1 - core) * half, half)
    copies = [
        pltpu.make_async_copy(near_hbm, a.at[pl.ds(own, half), :rank], sems.at[0]),
        pltpu.make_async_copy(far_hbm, a.at[pl.ds(others, half), :rank], sems.at[1]),
        pltpu.make_async_copy(z_hbm, a.at[:, rank:], sems.at[2]),
    ]
    for copy in copies:
        copy.start()
    for copy in copies:
        copy.wait()
    step, pair = LANES, 2 * LANES
    rc = ((1,), (0,))

    @pl.loop(0, rank // step)
    def _(j):
        r0 = pl.multiple_of(j * step, step)
        slot = pl.multiple_of(lax.rem(j, 2) * step, step)
        for t, panel in enumerate(inverse_factor(a[pl.ds(r0, step), pl.ds(r0, step)])):
            linv[TILE * t : TILE * (t + 1), :] = panel
        inverse = linv[...]
        y = dot(inverse, a[pl.ds(r0, step), rank:], rc)
        y_ref[pl.ds(r0, step), :] = y
        u[pl.ds(slot, step), rank:] = y

        @pl.loop(j + 1, rank // step)
        def _(c):
            at = pl.multiple_of(c * step, step)
            u[pl.ds(slot, step), pl.ds(at, step)] = dot(inverse, a[pl.ds(r0, step), pl.ds(at, step)], rc)

        @pl.when(lax.rem(j, 2) == 0)
        def _():
            r1 = pl.multiple_of((j + 1) * step, step)
            ut = u[pl.ds(0, step), pl.ds(r1, step)].T
            a[pl.ds(r1, step), rank:] -= dot(ut, y, rc)

            @pl.loop(j + 1, rank // step)
            def _(c):
                at = pl.multiple_of(c * step, step)
                a[pl.ds(r1, step), pl.ds(at, step)] -= dot(ut, u[pl.ds(0, step), pl.ds(at, step)], rc)

        @pl.when(lax.rem(j, 2) == 1)
        def _():
            @pl.loop((j + 1) // 2, rank // pair)
            def _(i):
                r1 = pl.multiple_of(i * pair, pair)
                ut = u[:, pl.ds(r1, pair)].T
                a[pl.ds(r1, pair), rank:] -= dot(ut, u[:, rank:], rc)

                @pl.loop(i, rank // pair)
                def _(c):
                    at = pl.multiple_of(c * pair, pair)
                    a[pl.ds(r1, pair), pl.ds(at, pair)] -= dot(ut, u[:, pl.ds(at, pair)], rc)


def factor_solve(core, near, far, rhs):
    rank, wide = rhs.shape
    return pl.pallas_call(
        solve_kernel,
        out_shape=jax.ShapeDtypeStruct((rank, wide), f32),
        in_specs=[pl.BlockSpec(memory_space=pltpu.SMEM)] + [pl.BlockSpec(memory_space=pl.ANY)] * 3,
        out_specs=pl.BlockSpec(memory_space=pltpu.VMEM),
        scratch_shapes=[
            pltpu.VMEM((rank, rank + wide), f32),
            pltpu.VMEM((LANES, LANES), f32),
            pltpu.VMEM((2 * LANES, rank + wide), f32),
            pltpu.SemaphoreType.DMA((3,)),
        ],
        compiler_params=pltpu.CompilerParams(vmem_limit_bytes=VMEM_LIMIT),
        name="factor_solve",
    )(core[None], near, far, rhs)


def shards(gradients, error_memory, q_factor):
    core = lax.axis_index(CORE)
    n_chips = lax.axis_size(CHIPS)
    n_dp = 2 * n_chips
    n_sh = lax.axis_size(SHARD)
    rows, cols = gradients.shape[1:]
    rank = q_factor.shape[1]
    own = -(-rows // (n_dp * LANES)) * LANES
    wide = -(-cols // (n_dp * TILE)) * n_dp * TILE
    gradient_t, error_t = gradients[0].T, error_memory[0].T

    with jax.named_scope("total"):
        mine, other = cut(core, gradient_t, error_t, n_chips, own)
        got = lax.ppermute(other, CORE, SWAP)
        pair = (mine.astype(f32) + got.astype(f32)).astype(bf16)
        arrived = lax.all_to_all(pair, CHIPS, 0, 0, tiled=True)
        total_t = jnp.sum(arrived.astype(f32), axis=0)

    with jax.named_scope("left"):
        part = dot(q_factor.astype(f32), total_t, ((0,), (0,)))
        arrived = lax.all_to_all(part.reshape(n_sh, rank // n_sh, own), SHARD, 0, 0, tiled=True)
        p_own = jnp.sum(arrived, axis=0)
        p_t = spread(p_own, SHARD, n_sh).reshape(n_sh, 2, rank // n_sh // 2, own)
        p_t = p_t.swapaxes(0, 1).reshape(rank, own)

    with jax.named_scope("gram"):
        g_rows = rank // n_sh // n_dp
        w_rows = wide // n_dp
        gram_part = dot(p_own, p_t, ((1,), (1,))).reshape(2, n_chips, g_rows, rank)
        w_part = jnp.pad(dot(total_t, p_t, ((1,), (1,))), ((0, wide - cols), (0, 0)))
        w_part = w_part.reshape(n_chips, 2, w_rows, rank)
        blocks = jnp.concatenate([gram_part.swapaxes(0, 1), w_part], axis=2)
        mine, other = halves(blocks, core)
        got = lax.ppermute(other, CORE, SWAP)
        arrived = lax.all_to_all(mine + got, CHIPS, 0, 0, tiled=True)
        summed = jnp.sum(arrived, axis=0)
        near = spread(summed[:g_rows], SHARD + CHIPS, n_sh * n_chips).reshape(rank // 2, rank)
        far = lax.ppermute(near, CORE, SWAP)

    with jax.named_scope("solve"):
        rhs = jnp.concatenate([p_t, jnp.pad(summed[g_rows:].T, ((0, 0), (0, LANES - w_rows)))], axis=1)
        solved = factor_solve(core, near, far, rhs)
        basis_t = solved[:, :own].astype(bf16)
        q_own = (solved[:, own : own + w_rows].T / n_dp).astype(bf16)

    with jax.named_scope("rebuild"):
        q_new = spread(q_own, DP, n_dp).reshape(wide, rank)
        block = dot(q_new[:cols], basis_t, ((1,), (0,)), None).astype(bf16)
        near = spread(block, CHIPS, n_chips)
        far = lax.ppermute(near, CORE, SWAP)
        rebuilt_t, new_error_t = finish(core, near, far, gradient_t, error_t)
    return (rebuilt_t.T, new_error_t.T[None])


def solution(mesh):
    fine = Mesh(mesh.devices.reshape(4, 2, 2, 2, 4), ("x", "yh", "c", "yl", "z"))
    in_specs = (P(DP, None, SHARD), P(DP, None, SHARD), P(SHARD, None))
    out_specs = (P(None, SHARD), P(DP, None, SHARD))
    return jax.shard_map(shards, mesh=fine, in_specs=in_specs, out_specs=out_specs, check_vma=False)
```

```python
import functools

import jax
import jax.numpy as jnp
from jax import lax
from jax.experimental import pallas as pl
from jax.experimental.pallas import tpu as pltpu
from jax.sharding import Mesh, PartitionSpec as P

f32 = jnp.float32
bf16 = jnp.bfloat16
HIGHEST = lax.Precision.HIGHEST

CHIPS = ("x", "yh")
CORE = "c"
SHARD = ("yl", "z")
DP = CHIPS + (CORE,)
SWAP = [(0, 1), (1, 0)]

TILE, LANES = 8, 128
VMEM_LIMIT = 48 * 2**20


def dot(a, b, dims, precision=HIGHEST):
    return lax.dot_general(a, b, (dims, ((), ())), precision=precision, preferred_element_type=f32)


def spread(a, axes, n):
    blocks = jnp.broadcast_to(a[None], (n,) + a.shape)
    return lax.all_to_all(blocks, axes, 0, 0, tiled=True)


def halves(blocks, core):
    first = core == 0
    return (
        jnp.where(first, blocks[:, 0], blocks[:, 1]),
        jnp.where(first, blocks[:, 1], blocks[:, 0]),
    )


def cut_kernel(rows, core_ref, g_ref, e_ref, mine_ref, other_ref):
    core = core_ref[0]
    width = mine_ref.shape[2]
    combined = g_ref[...].astype(f32) + e_ref[...]
    at = pl.program_id(0) * 2 * width + lax.broadcasted_iota(jnp.int32, combined.shape, 1)
    combined = jnp.where(at < rows, combined, 0.0).astype(bf16)
    low, high = combined[:, :width], combined[:, width:]

    @pl.when(core == 0)
    def _():
        mine_ref[0], other_ref[0] = low, high

    @pl.when(core != 0)
    def _():
        mine_ref[0], other_ref[0] = high, low


def cut(core, gradient_t, error_t, n_chips, width):
    cols, rows = gradient_t.shape
    whole = pl.BlockSpec((cols, 2 * width), lambda i, core: (0, i))
    part = pl.BlockSpec((1, cols, width), lambda i, core: (i, 0, 0))
    shape = jax.ShapeDtypeStruct((n_chips, cols, width), bf16)
    return pl.pallas_call(
        functools.partial(cut_kernel, rows),
        grid_spec=pltpu.PrefetchScalarGridSpec(
            num_scalar_prefetch=1, grid=(n_chips,), in_specs=[whole, whole], out_specs=[part, part]
        ),
        out_shape=[shape, shape],
        compiler_params=pltpu.CompilerParams(vmem_limit_bytes=VMEM_LIMIT),
        name="cut",
    )(core[None], gradient_t, error_t)


def finish_kernel(core_ref, near_ref, far_ref, x_near_ref, x_far_ref, g_ref, e_ref, rebuilt_ref, error_ref, x):
    core = core_ref[0]
    width = near_ref.shape[2]
    cols = g_ref.shape[0]
    n_chips, _, band, _ = x_near_ref.shape

    @pl.when(pl.program_id(0) == 0)
    def _():
        for i in range(n_chips):
            own = pl.multiple_of((2 * i + core) * band, band)
            others = pl.multiple_of((2 * i + 1 - core) * band, band)
            for part in range(2):
                x[part, pl.ds(own, band)] = x_near_ref[i, part]
                x[part, pl.ds(others, band)] = x_far_ref[i, part]

    def store(columns, block):
        value = dot(x[0, :cols], block, ((1,), (0,)), None) + dot(x[1, :cols], block, ((1,), (0,)), None)
        rebuilt_ref[:, columns] = value.astype(bf16)
        error_ref[:, columns] = g_ref[:, columns].astype(f32) + e_ref[:, columns] - value

    low, high = pl.ds(0, width), pl.ds(width, width)

    @pl.when(core == 0)
    def _():
        store(low, near_ref[0])
        store(high, far_ref[0])

    @pl.when(core != 0)
    def _():
        store(low, far_ref[0])
        store(high, near_ref[0])


def finish(core, near, far, x_near, x_far, gradient_t, error_t):
    cols, rows = gradient_t.shape
    n_chips, rank, width = near.shape
    whole = pl.BlockSpec((cols, 2 * width), lambda i, core: (0, i))
    part = pl.BlockSpec((1, rank, width), lambda i, core: (i, 0, 0))
    fixed = pl.BlockSpec(x_near.shape, lambda i, core: (0, 0, 0, 0))
    return pl.pallas_call(
        finish_kernel,
        grid_spec=pltpu.PrefetchScalarGridSpec(
            num_scalar_prefetch=1,
            grid=(n_chips,),
            in_specs=[part, part, fixed, fixed, whole, whole],
            out_specs=[whole, whole],
            scratch_shapes=[pltpu.VMEM((2, n_chips * 2 * x_near.shape[2], rank), bf16)],
        ),
        out_shape=[
            jax.ShapeDtypeStruct((cols, rows), bf16),
            jax.ShapeDtypeStruct((cols, rows), f32),
        ],
        compiler_params=pltpu.CompilerParams(vmem_limit_bytes=VMEM_LIMIT),
        name="finish",
    )(core[None], near, far, x_near, x_far, gradient_t, error_t)


def inverse_factor(block):
    n = LANES // TILE
    sub = lax.broadcasted_iota(jnp.int32, (TILE, LANES), 0)
    lane = lax.broadcasted_iota(jnp.int32, (TILE, LANES), 1)
    left = [block[TILE * t : TILE * (t + 1)] for t in range(n)]
    right = [jnp.where(lane == sub + TILE * t, 1.0, 0.0).astype(f32) for t in range(n)]
    full = lambda v: jnp.broadcast_to(v, (TILE, LANES))
    out = []
    for t in range(n):
        at = TILE * t
        rows_l = [full(left[t][k : k + 1]) for k in range(TILE)]
        rows_r = [full(right[t][k : k + 1]) for k in range(TILE)]
        cols = [full(left[t][:, at + k : at + k + 1]) for k in range(TILE)]
        s = [[full(cols[k][i : i + 1]) for k in range(i + 1)] for i in range(TILE)]
        later = range(t + 1, n)
        e = {p: [full(left[p][:, at + k : at + k + 1]) for k in range(TILE)] for p in later}
        pivots = result = None
        for k in range(TILE):
            d = s[k][k]
            inv = 1.0 / d
            l = {i: s[i][k] * inv for i in range(k + 1, TILE)}
            for i in range(k + 1, TILE):
                for m in range(k + 1, i + 1):
                    s[i][m] = s[i][m] - l[i] * s[m][k]
            scaled_l, scaled_r = rows_l[k] * inv, rows_r[k] * inv
            for i in range(k + 1, TILE):
                rows_l[i] = rows_l[i] - l[i] * rows_l[k]
                rows_r[i] = rows_r[i] - l[i] * rows_r[k]
            for p in later:
                left[p] = left[p] - e[p][k] * scaled_l
                right[p] = right[p] - e[p][k] * scaled_r
                for i in range(k + 1, TILE):
                    e[p][i] = e[p][i] - l[i] * e[p][k]
            pivots = d if k == 0 else jnp.where(sub == k, d, pivots)
            result = rows_r[k] if k == 0 else jnp.where(sub == k, rows_r[k], result)
        out.append(result * lax.rsqrt(pivots))
    return out


def factor_kernel(core_ref, near_hbm, far_hbm, u_ref, inverse_ref, a, sems):
    half, rank = near_hbm.shape
    core = core_ref[0]
    own = pl.multiple_of(core * half, half)
    others = pl.multiple_of((1 - core) * half, half)
    copies = [
        pltpu.make_async_copy(near_hbm, a.at[pl.ds(own, half)], sems.at[0]),
        pltpu.make_async_copy(far_hbm, a.at[pl.ds(others, half)], sems.at[1]),
    ]
    for copy in copies:
        copy.start()
    for copy in copies:
        copy.wait()
    step, pair = LANES, 2 * LANES
    rc = ((1,), (0,))

    @pl.loop(0, rank // step)
    def _(j):
        r0 = pl.multiple_of(j * step, step)
        side = pl.multiple_of(lax.rem(j, 2) * step, step)
        for t, panel in enumerate(inverse_factor(a[pl.ds(r0, step), pl.ds(r0, step)])):
            inverse_ref[pl.ds(pl.multiple_of(r0 + TILE * t, TILE), TILE), pl.ds(side, step)] = panel
        inverse = inverse_ref[pl.ds(r0, step), pl.ds(side, step)]

        @pl.loop(j + 1, rank // step)
        def _(c):
            at = pl.multiple_of(c * step, step)
            u_ref[pl.ds(r0, step), pl.ds(at, step)] = dot(inverse, a[pl.ds(r0, step), pl.ds(at, step)], rc)

        @pl.when(lax.rem(j, 2) == 0)
        def _():
            r1 = pl.multiple_of((j + 1) * step, step)
            ut = u_ref[pl.ds(r0, step), pl.ds(r1, step)].T
            inverse_ref[pl.ds(r0, step), step:] = jnp.zeros((step, step), f32)

            @pl.loop(j + 1, rank // step)
            def _(c):
                at = pl.multiple_of(c * step, step)
                a[pl.ds(r1, step), pl.ds(at, step)] -= dot(ut, u_ref[pl.ds(r0, step), pl.ds(at, step)], rc)

        @pl.when(lax.rem(j, 2) == 1)
        def _():
            p0 = pl.multiple_of((j - 1) * step, pair)
            before = inverse_ref[pl.ds(p0, step), :step]
            cross = dot(u_ref[pl.ds(p0, step), pl.ds(r0, step)], before, ((0,), (0,)))
            inverse_ref[pl.ds(r0, step), :step] = -dot(inverse, cross, rc)

            @pl.loop((j + 1) // 2, rank // pair)
            def _(i):
                r1 = pl.multiple_of(i * pair, pair)
                ut = u_ref[pl.ds(p0, pair), pl.ds(r1, pair)].T

                @pl.loop(i, rank // pair)
                def _(c):
                    at = pl.multiple_of(c * pair, pair)
                    a[pl.ds(r1, pair), pl.ds(at, pair)] -= dot(ut, u_ref[pl.ds(p0, pair), pl.ds(at, pair)], rc)


def factor(core, near, far):
    half, rank = near.shape
    return pl.pallas_call(
        factor_kernel,
        out_shape=[
            jax.ShapeDtypeStruct((rank, rank), f32),
            jax.ShapeDtypeStruct((rank, 2 * LANES), f32),
        ],
        in_specs=[pl.BlockSpec(memory_space=pltpu.SMEM)] + [pl.BlockSpec(memory_space=pl.ANY)] * 2,
        out_specs=[pl.BlockSpec(memory_space=pltpu.VMEM)] * 2,
        scratch_shapes=[pltpu.VMEM((rank, rank), f32), pltpu.SemaphoreType.DMA((2,))],
        compiler_params=pltpu.CompilerParams(vmem_limit_bytes=VMEM_LIMIT),
        cost_estimate=pl.CostEstimate(flops=60_000_000_000, bytes_accessed=8 * rank * rank, transcendentals=0),
        name="factor",
    )(core[None], near, far)


def solve_kernel(scale, w_ref, u_ref, inverse_ref, x_ref, y, x):
    pair = 2 * LANES
    n = w_ref.shape[1] // pair
    block = lambda j: slice(j * pair, (j + 1) * pair)
    for j in range(n):
        value = w_ref[:, block(j)]
        if j:
            value = value - dot(y[:, : j * pair], u_ref[: j * pair, block(j)], ((1,), (0,)))
        y[:, block(j)] = dot(value, inverse_ref[block(j), :], ((1,), (1,)))
    for j in reversed(range(n)):
        value = y[:, block(j)]
        if j < n - 1:
            value = value - dot(x[:, (j + 1) * pair :], u_ref[block(j), (j + 1) * pair :], ((1,), (1,)))
        x[:, block(j)] = dot(value, inverse_ref[block(j), :], ((1,), (0,)))
    scaled = x[...] * scale
    high = scaled.astype(bf16)
    x_ref[0] = high
    x_ref[1] = (scaled - high.astype(f32)).astype(bf16)


def solve(w, u, inverse, scale):
    return pl.pallas_call(
        functools.partial(solve_kernel, scale),
        out_shape=jax.ShapeDtypeStruct((2,) + w.shape, bf16),
        in_specs=[pl.BlockSpec(memory_space=pltpu.VMEM)] * 3,
        out_specs=pl.BlockSpec(memory_space=pltpu.VMEM),
        scratch_shapes=[pltpu.VMEM(w.shape, f32), pltpu.VMEM(w.shape, f32)],
        compiler_params=pltpu.CompilerParams(vmem_limit_bytes=VMEM_LIMIT),
        cost_estimate=pl.CostEstimate(flops=8_000_000_000, bytes_accessed=16 * 2**20, transcendentals=0),
        name="solve",
    )(w, u, inverse)


def shards(gradients, error_memory, q_factor):
    core = lax.axis_index(CORE)
    n_chips = lax.axis_size(CHIPS)
    n_dp = 2 * n_chips
    n_sh = lax.axis_size(SHARD)
    rows, cols = gradients.shape[1:]
    rank = q_factor.shape[1]
    own = -(-rows // (n_dp * LANES)) * LANES
    wide = -(-cols // (n_dp * 16)) * n_dp * 16
    gradient_t, error_t = gradients[0].T, error_memory[0].T

    with jax.named_scope("total"):
        mine, other = cut(core, gradient_t, error_t, n_chips, own)
        got = lax.ppermute(other, CORE, SWAP)
        pair = (mine.astype(f32) + got.astype(f32)).astype(bf16)
        arrived = lax.all_to_all(pair, CHIPS, 0, 0, tiled=True)
        total_t = jnp.sum(arrived.astype(f32), axis=0)

    with jax.named_scope("left"):
        part = dot(q_factor.astype(f32), total_t, ((0,), (0,)))
        arrived = lax.all_to_all(part.reshape(n_sh, rank // n_sh, own), SHARD, 0, 0, tiled=True)
        p_own = jnp.sum(arrived, axis=0).astype(bf16)
        p_t = spread(p_own, SHARD, n_sh).reshape(n_sh, 2, rank // n_sh // 2, own)
        p_t = p_t.swapaxes(0, 1).reshape(rank, own)

    with jax.named_scope("gram"):
        g_rows = rank // n_sh // n_dp
        w_rows = wide // n_dp
        gram_part = dot(p_own, p_t, ((1,), (1,)), None).reshape(2, n_chips, g_rows, rank)
        w_part = jnp.pad(dot(total_t, p_t.astype(f32), ((1,), (1,))), ((0, wide - cols), (0, 0)))
        w_part = w_part.reshape(n_chips, 2, w_rows, rank)
        mine, other = halves(jnp.concatenate([gram_part.swapaxes(0, 1), w_part], axis=2), core)
        got = lax.ppermute(other, CORE, SWAP)
        arrived = lax.all_to_all(mine + got, CHIPS, 0, 0, tiled=True)
        summed = jnp.sum(arrived, axis=0)
        near = spread(summed[:g_rows], SHARD + CHIPS, n_sh * n_chips).reshape(rank // 2, rank)
        far = lax.ppermute(near, CORE, SWAP)

    with jax.named_scope("solve"):
        near, far, p_t = lax.optimization_barrier((near, far, p_t))
        p_near = spread(p_t, CHIPS, n_chips)
        u, inverse = factor(core, near, far)
        p_near, u, inverse = lax.optimization_barrier((p_near, u, inverse))
        p_far = lax.ppermute(p_near, CORE, SWAP)
        x_own = solve(summed[g_rows:], u, inverse, 1.0 / n_dp)

    with jax.named_scope("rebuild"):
        x_near = spread(x_own, CHIPS, n_chips)
        x_far = lax.ppermute(x_near, CORE, SWAP)
        rebuilt_t, new_error_t = finish(core, p_near, p_far, x_near, x_far, gradient_t, error_t)
    return (rebuilt_t.T, new_error_t.T[None])


def solution(mesh):
    fine = Mesh(mesh.devices.reshape(4, 2, 2, 2, 4), ("x", "yh", "c", "yl", "z"))
    in_specs = (P(DP, None, SHARD), P(DP, None, SHARD), P(SHARD, None))
    out_specs = (P(None, SHARD), P(DP, None, SHARD))
    return jax.shard_map(shards, mesh=fine, in_specs=in_specs, out_specs=out_specs, check_vma=False)
```

```python
import functools

import jax
import jax.numpy as jnp
from jax import lax
from jax.experimental import pallas as pl
from jax.experimental.pallas import tpu as pltpu
from jax.sharding import Mesh, PartitionSpec as P

f32 = jnp.float32
bf16 = jnp.bfloat16
HIGHEST = lax.Precision.HIGHEST

CHIPS = ("x", "yh")
CORE = "c"
SHARD = ("yl", "z")
DP = CHIPS + (CORE,)
SWAP = [(0, 1), (1, 0)]

TILE, LANES = 8, 128
VMEM_LIMIT = 48 * 2**20


def dot(a, b, dims, precision=HIGHEST):
    return lax.dot_general(a, b, (dims, ((), ())), precision=precision, preferred_element_type=f32)


def spread(a, axes, n):
    blocks = jnp.broadcast_to(a[None], (n,) + a.shape)
    return lax.all_to_all(blocks, axes, 0, 0, tiled=True)


def cut_kernel(rows, core_ref, g_ref, e_ref, mine_ref, other_ref):
    core = core_ref[0]
    width = mine_ref.shape[2]
    combined = g_ref[...].astype(f32) + e_ref[...]
    at = pl.program_id(0) * 2 * width + lax.broadcasted_iota(jnp.int32, combined.shape, 1)
    combined = jnp.where(at < rows, combined, 0.0).astype(bf16)
    low, high = combined[:, :width], combined[:, width:]

    @pl.when(core == 0)
    def _():
        mine_ref[0], other_ref[0] = low, high

    @pl.when(core != 0)
    def _():
        mine_ref[0], other_ref[0] = high, low


def cut(core, gradient_t, error_t, n_chips, width):
    cols, rows = gradient_t.shape
    whole = pl.BlockSpec((cols, 2 * width), lambda i, core: (0, i))
    part = pl.BlockSpec((1, cols, width), lambda i, core: (i, 0, 0))
    shape = jax.ShapeDtypeStruct((n_chips, cols, width), bf16)
    return pl.pallas_call(
        functools.partial(cut_kernel, rows),
        grid_spec=pltpu.PrefetchScalarGridSpec(
            num_scalar_prefetch=1, grid=(n_chips,), in_specs=[whole, whole], out_specs=[part, part]
        ),
        out_shape=[shape, shape],
        compiler_params=pltpu.CompilerParams(vmem_limit_bytes=VMEM_LIMIT),
        name="cut",
    )(core[None], gradient_t, error_t)


def finish_kernel(core_ref, near_ref, far_ref, x_near_ref, x_far_ref, g_ref, e_ref, rebuilt_ref, error_ref, x):
    core = core_ref[0]
    n_sh, _, depth, width = near_ref.shape
    cols = g_ref.shape[0]
    n_chips, band, _ = x_near_ref.shape

    @pl.when(pl.program_id(0) == 0)
    def _():
        for i in range(n_chips):
            x[pl.ds(pl.multiple_of((2 * i + core) * band, band), band)] = x_near_ref[i]
            x[pl.ds(pl.multiple_of((2 * i + 1 - core) * band, band), band)] = x_far_ref[i]

    def store(columns, ref):
        value = dot(x[:cols], ref[:, 0].reshape(n_sh * depth, width), ((1,), (0,)), None)
        rebuilt_ref[:, columns] = value.astype(bf16)
        error_ref[:, columns] = g_ref[:, columns].astype(f32) + e_ref[:, columns] - value

    low, high = pl.ds(0, width), pl.ds(width, width)

    @pl.when(core == 0)
    def _():
        store(low, near_ref)
        store(high, far_ref)

    @pl.when(core != 0)
    def _():
        store(low, far_ref)
        store(high, near_ref)


def finish(core, near, far, x_near, x_far, gradient_t, error_t):
    cols, rows = gradient_t.shape
    n_sh, n_chips, depth, width = near.shape
    whole = pl.BlockSpec((cols, 2 * width), lambda i, core: (0, i))
    part = pl.BlockSpec((n_sh, 1, depth, width), lambda i, core: (0, i, 0, 0))
    fixed = pl.BlockSpec(x_near.shape, lambda i, core: (0, 0, 0))
    return pl.pallas_call(
        finish_kernel,
        grid_spec=pltpu.PrefetchScalarGridSpec(
            num_scalar_prefetch=1,
            grid=(n_chips,),
            in_specs=[part, part, fixed, fixed, whole, whole],
            out_specs=[whole, whole],
            scratch_shapes=[pltpu.VMEM((n_chips * 2 * x_near.shape[1], x_near.shape[2]), bf16)],
        ),
        out_shape=[
            jax.ShapeDtypeStruct((cols, rows), bf16),
            jax.ShapeDtypeStruct((cols, rows), f32),
        ],
        compiler_params=pltpu.CompilerParams(vmem_limit_bytes=VMEM_LIMIT),
        name="finish",
    )(core[None], near, far, x_near, x_far, gradient_t, error_t)


def add_gram(p, g_ref):
    wide = 2 * LANES
    for i in range(0, p.shape[0], wide):
        g_ref[i : i + wide, i:] += dot(p[i : i + wide], p[i:], ((1,), (1,)), None)


def inverse_factor(block, held):
    n = LANES // TILE
    sub = lax.broadcasted_iota(jnp.int32, (TILE, LANES), 0)
    lane = lax.broadcasted_iota(jnp.int32, (TILE, LANES), 1)
    panel = [block[TILE * t : TILE * (t + 1)] for t in range(n)]
    full = lambda v: jnp.broadcast_to(v, (TILE, LANES))
    out = []
    for t in range(n):
        at = TILE * t
        pivot_lanes = (lane >= at) & (lane < at + TILE)
        column = lambda p: [full(panel[p][:, at + k : at + k + 1]) for k in range(TILE)]
        cols = column(t)
        for k in range(TILE):
            held[k] = cols[k]
        s = [[full(held[k, i : i + 1]) for k in range(i + 1)] for i in range(TILE)]
        later = range(t + 1, n)
        e = {p: column(p) for p in later}
        for p in later:
            panel[p] = jnp.where(pivot_lanes, 0.0, panel[p])
        own = jnp.where(pivot_lanes, jnp.where(lane == sub + at, 1.0, 0.0), panel[t])
        held[TILE] = own
        rows = [full(held[TILE, k : k + 1]) for k in range(TILE)]
        inv, low = [], []
        pivots = result = None
        for k in range(TILE):
            d = s[k][k]
            inv.append(1.0 / d)
            l = {i: s[i][k] * inv[k] for i in range(k + 1, TILE)}
            low.append(l)
            for i in range(k + 1, TILE):
                for m in range(k + 1, i + 1):
                    s[i][m] = s[i][m] - l[i] * s[m][k]
            for i in range(k + 1, TILE):
                rows[i] = rows[i] - l[i] * rows[k]
            if t + 1 < n:
                following = e[t + 1]
                panel[t + 1] = panel[t + 1] - following[k] * (rows[k] * inv[k])
                for i in range(k + 1, TILE):
                    following[i] = following[i] - l[i] * following[k]
            pivots = d if k == 0 else jnp.where(sub == k, d, pivots)
            result = rows[k] if k == 0 else jnp.where(sub == k, rows[k], result)
        out.append(jnp.where(lane < at + TILE, result * lax.rsqrt(pivots), 0.0))
        if t + 2 < n:
            v = [None] * TILE
            for k in reversed(range(TILE)):
                v[k] = rows[k] * inv[k]
                for i in range(k + 1, TILE):
                    v[k] = v[k] - low[k][i] * v[i]
            for p in later[1:]:
                for k in range(TILE):
                    panel[p] = panel[p] - e[p][k] * v[k]
    return out


def factor_kernel(near_hbm, far_hbm, u_hbm, inverse_ref, a, u_ref, near, far, held, sems, out_sems):
    n_sh, n_chips, depth, width = near_hbm.shape
    rank = n_sh * depth
    near_copy = pltpu.make_async_copy(near_hbm, near, sems.at[0])
    far_copy = pltpu.make_async_copy(far_hbm, far, sems.at[1])
    near_copy.start()
    far_copy.start()
    a[...] = jnp.zeros_like(a)
    near_copy.wait()

    @pl.loop(0, n_chips)
    def _(i):
        add_gram(near[:, i].reshape(rank, width), a)

    far_copy.wait()

    @pl.loop(0, n_chips)
    def _(i):
        add_gram(far[:, i].reshape(rank, width), a)

    step, pair = LANES, 2 * LANES
    rc = ((1,), (0,))

    def out_copy(j):
        band = pl.ds(pl.multiple_of(j * step, step), step)
        return pltpu.make_async_copy(u_ref.at[band], u_hbm.at[band], out_sems.at[j])

    @pl.loop(0, rank // step)
    def _(j):
        r0 = pl.multiple_of(j * step, step)
        side = pl.multiple_of(lax.rem(j, 2) * step, step)
        for t, panel in enumerate(inverse_factor(a[pl.ds(r0, step), pl.ds(r0, step)], held)):
            inverse_ref[pl.ds(pl.multiple_of(r0 + TILE * t, TILE), TILE), pl.ds(side, step)] = panel
        inverse = inverse_ref[pl.ds(r0, step), pl.ds(side, step)]

        @pl.loop((j + 1) // 2, rank // pair)
        def _(c):
            at = pl.multiple_of(c * pair, pair)
            u_ref[pl.ds(r0, step), pl.ds(at, pair)] = dot(inverse, a[pl.ds(r0, step), pl.ds(at, pair)], rc)

        out_copy(j).start()

        @pl.when(lax.rem(j, 2) == 0)
        def _():
            r1 = pl.multiple_of((j + 1) * step, step)
            ut = u_ref[pl.ds(r0, step), pl.ds(r1, step)].T
            inverse_ref[pl.ds(r0, step), step:] = jnp.zeros((step, step), f32)

            @pl.loop(j // 2, rank // pair)
            def _(c):
                at = pl.multiple_of(c * pair, pair)
                a[pl.ds(r1, step), pl.ds(at, pair)] -= dot(ut, u_ref[pl.ds(r0, step), pl.ds(at, pair)], rc)

        @pl.when(lax.rem(j, 2) == 1)
        def _():
            p0 = pl.multiple_of((j - 1) * step, pair)
            before = inverse_ref[pl.ds(p0, step), :step]
            cross = dot(u_ref[pl.ds(p0, step), pl.ds(r0, step)], before, ((0,), (0,)))
            inverse_ref[pl.ds(r0, step), :step] = -dot(inverse, cross, rc)

            @pl.loop((j + 1) // 2, rank // pair)
            def _(i):
                r1 = pl.multiple_of(i * pair, pair)
                ut = u_ref[pl.ds(p0, pair), pl.ds(r1, pair)].T

                @pl.loop(i, rank // pair)
                def _(c):
                    at = pl.multiple_of(c * pair, pair)
                    a[pl.ds(r1, pair), pl.ds(at, pair)] -= dot(ut, u_ref[pl.ds(p0, pair), pl.ds(at, pair)], rc)

    @pl.loop(0, rank // step)
    def _(j):
        out_copy(j).wait()


def factor(near, far):
    rank = near.shape[0] * near.shape[2]
    return pl.pallas_call(
        factor_kernel,
        out_shape=[
            jax.ShapeDtypeStruct((rank, rank), f32),
            jax.ShapeDtypeStruct((rank, 2 * LANES), f32),
        ],
        in_specs=[pl.BlockSpec(memory_space=pl.ANY)] * 2,
        out_specs=[pl.BlockSpec(memory_space=pl.ANY), pl.BlockSpec(memory_space=pltpu.VMEM)],
        scratch_shapes=[
            pltpu.VMEM((rank, rank), f32),
            pltpu.VMEM((rank, rank), f32),
            pltpu.VMEM(near.shape, bf16),
            pltpu.VMEM(far.shape, bf16),
            pltpu.VMEM((TILE + 1, TILE, LANES), f32),
            pltpu.SemaphoreType.DMA((2,)),
            pltpu.SemaphoreType.DMA((rank // LANES,)),
        ],
        compiler_params=pltpu.CompilerParams(vmem_limit_bytes=VMEM_LIMIT),
        cost_estimate=pl.CostEstimate(flops=60_000_000_000, bytes_accessed=8 * rank * rank, transcendentals=0),
        name="factor",
    )(near, far)


def solve_kernel(scale, parts_ref, u_ref, inverse_ref, x_ref, w, y):
    pair = 2 * LANES
    rank = u_ref.shape[0]
    n = rank // pair
    block = lambda j: slice(j * pair, (j + 1) * pair)
    w[...] = sum(parts_ref[i] for i in range(parts_ref.shape[0]))
    for j in range(n):
        value = w[:, block(j)]
        if j:
            value = value - dot(y[:, : j * pair], u_ref[: j * pair, block(j)], ((1,), (0,)))
        y[:, block(j)] = dot(value, inverse_ref[block(j), :], ((1,), (1,)))
    for j in reversed(range(n)):
        value = y[:, block(j)]
        if j < n - 1:
            value = value - dot(w[:, (j + 1) * pair :], u_ref[block(j), (j + 1) * pair :], ((1,), (1,)))
        x = dot(value, inverse_ref[block(j), :], ((1,), (0,)))
        w[:, block(j)] = x
        x_ref[:, block(j)] = (x * scale).astype(bf16)


def solve(parts, u, inverse, scale):
    shape = parts.shape[1:]
    return pl.pallas_call(
        functools.partial(solve_kernel, scale),
        out_shape=jax.ShapeDtypeStruct(shape, bf16),
        in_specs=[pl.BlockSpec(memory_space=pltpu.VMEM)] * 3,
        out_specs=pl.BlockSpec(memory_space=pltpu.VMEM),
        scratch_shapes=[pltpu.VMEM(shape, f32), pltpu.VMEM(shape, f32)],
        compiler_params=pltpu.CompilerParams(vmem_limit_bytes=VMEM_LIMIT),
        cost_estimate=pl.CostEstimate(flops=8_000_000_000, bytes_accessed=16 * 2**20, transcendentals=0),
        name="solve",
    )(parts, u, inverse)


def shards(gradients, error_memory, q_factor):
    core = lax.axis_index(CORE)
    n_chips = lax.axis_size(CHIPS)
    n_dp = 2 * n_chips
    n_sh = lax.axis_size(SHARD)
    rows, cols = gradients.shape[1:]
    rank = q_factor.shape[1]
    own = -(-rows // (n_dp * LANES)) * LANES
    wide = -(-cols // (n_dp * 16)) * n_dp * 16
    gradient_t, error_t = gradients[0].T, error_memory[0].T

    with jax.named_scope("total"):
        mine, other = cut(core, gradient_t, error_t, n_chips, own)
        got = lax.ppermute(other, CORE, SWAP)
        pair = (mine.astype(f32) + got.astype(f32)).astype(bf16)
        arrived = lax.all_to_all(pair, CHIPS, 0, 0, tiled=True)
        total_t = jnp.sum(arrived.astype(f32), axis=0)

    with jax.named_scope("left"):
        part = dot(q_factor.astype(f32), total_t, ((0,), (0,)))
        arrived = lax.all_to_all(part.reshape(n_sh, rank // n_sh, own), SHARD, 0, 0, tiled=True)
        p_own = jnp.sum(arrived, axis=0).astype(bf16)
        p_near = spread(p_own, SHARD + CHIPS, n_sh * n_chips).reshape(n_sh, n_chips, rank // n_sh, own)
        p_far = lax.ppermute(p_near, CORE, SWAP)

    with jax.named_scope("right"):
        p_t = lax.dynamic_index_in_dim(p_near, lax.axis_index(CHIPS), 1, keepdims=False).reshape(rank, own)
        total_wide = jnp.pad(total_t, ((0, wide - cols), (0, 0)))
        w_part = dot(total_wide, p_t.astype(f32), ((1,), (1,)))
        w_parts = lax.all_to_all(w_part.reshape(n_dp, wide // n_dp, rank), DP, 0, 0, tiled=True)

    with jax.named_scope("solve"):
        u, inverse = factor(p_near, p_far)
        x_own = solve(w_parts, u, inverse, 1.0 / n_dp)

    with jax.named_scope("rebuild"):
        x_near = spread(x_own, CHIPS, n_chips)
        x_far = lax.ppermute(x_near, CORE, SWAP)
        rebuilt_t, new_error_t = finish(core, p_near, p_far, x_near, x_far, gradient_t, error_t)
    return (rebuilt_t.T, new_error_t.T[None])


def solution(mesh):
    fine = Mesh(mesh.devices.reshape(4, 2, 2, 2, 4), ("x", "yh", "c", "yl", "z"))
    in_specs = (P(DP, None, SHARD), P(DP, None, SHARD), P(SHARD, None))
    out_specs = (P(None, SHARD), P(DP, None, SHARD))
    return jax.shard_map(shards, mesh=fine, in_specs=in_specs, out_specs=out_specs, check_vma=False)
```

```python
import functools

import jax
import jax.numpy as jnp
from jax import lax
from jax.experimental import pallas as pl
from jax.experimental.pallas import tpu as pltpu
from jax.sharding import Mesh, PartitionSpec as P

f32 = jnp.float32
bf16 = jnp.bfloat16
HIGHEST = lax.Precision.HIGHEST
HIGH = lax.Precision.HIGH

CHIPS = ("x", "yh")
CORE = "c"
SHARD = ("yl", "z")
DP = CHIPS + (CORE,)
SWAP = [(0, 1), (1, 0)]

TILE, LANES = 8, 128
VMEM_LIMIT = 48 * 2**20


def dot(a, b, dims, precision=HIGHEST):
    return lax.dot_general(a, b, (dims, ((), ())), precision=precision, preferred_element_type=f32)


def spread(a, axes, n):
    blocks = jnp.broadcast_to(a[None], (n,) + a.shape)
    return lax.all_to_all(blocks, axes, 0, 0, tiled=True)


def cut_kernel(rows, core_ref, g_ref, e_ref, mine_ref, other_ref):
    core = core_ref[0]
    width = mine_ref.shape[2]
    combined = g_ref[...].astype(f32) + e_ref[...]
    at = pl.program_id(0) * 2 * width + lax.broadcasted_iota(jnp.int32, combined.shape, 1)
    combined = jnp.where(at < rows, combined, 0.0).astype(bf16)
    low, high = combined[:, :width], combined[:, width:]

    @pl.when(core == 0)
    def _():
        mine_ref[0], other_ref[0] = low, high

    @pl.when(core != 0)
    def _():
        mine_ref[0], other_ref[0] = high, low


def cut(core, gradient_t, error_t, n_chips, width):
    cols, rows = gradient_t.shape
    whole = pl.BlockSpec((cols, 2 * width), lambda i, core: (0, i))
    part = pl.BlockSpec((1, cols, width), lambda i, core: (i, 0, 0))
    shape = jax.ShapeDtypeStruct((n_chips, cols, width), bf16)
    return pl.pallas_call(
        functools.partial(cut_kernel, rows),
        grid_spec=pltpu.PrefetchScalarGridSpec(
            num_scalar_prefetch=1, grid=(n_chips,), in_specs=[whole, whole], out_specs=[part, part]
        ),
        out_shape=[shape, shape],
        compiler_params=pltpu.CompilerParams(vmem_limit_bytes=VMEM_LIMIT),
        name="cut",
    )(core[None], gradient_t, error_t)


def finish_kernel(core_ref, near_ref, far_ref, x_near_ref, x_far_ref, g_ref, e_ref, rebuilt_ref, error_ref, x):
    core = core_ref[0]
    n_sh, _, depth, width = near_ref.shape
    cols = g_ref.shape[0]
    n_chips, band, _ = x_near_ref.shape

    @pl.when(pl.program_id(0) == 0)
    def _():
        for i in range(n_chips):
            x[pl.ds(pl.multiple_of((2 * i + core) * band, band), band)] = x_near_ref[i]
            x[pl.ds(pl.multiple_of((2 * i + 1 - core) * band, band), band)] = x_far_ref[i]

    def store(columns, ref):
        value = dot(x[:cols], ref[:, 0].reshape(n_sh * depth, width), ((1,), (0,)), None)
        rebuilt_ref[:, columns] = value.astype(bf16)
        error_ref[:, columns] = g_ref[:, columns].astype(f32) + e_ref[:, columns] - value

    low, high = pl.ds(0, width), pl.ds(width, width)

    @pl.when(core == 0)
    def _():
        store(low, near_ref)
        store(high, far_ref)

    @pl.when(core != 0)
    def _():
        store(low, far_ref)
        store(high, near_ref)


def finish(core, near, far, x_near, x_far, gradient_t, error_t):
    cols, rows = gradient_t.shape
    n_sh, n_chips, depth, width = near.shape
    whole = pl.BlockSpec((cols, 2 * width), lambda i, core: (0, i))
    part = pl.BlockSpec((n_sh, 1, depth, width), lambda i, core: (0, i, 0, 0))
    fixed = pl.BlockSpec(x_near.shape, lambda i, core: (0, 0, 0))
    return pl.pallas_call(
        finish_kernel,
        grid_spec=pltpu.PrefetchScalarGridSpec(
            num_scalar_prefetch=1,
            grid=(n_chips,),
            in_specs=[part, part, fixed, fixed, whole, whole],
            out_specs=[whole, whole],
            scratch_shapes=[pltpu.VMEM((n_chips * 2 * x_near.shape[1], x_near.shape[2]), bf16)],
        ),
        out_shape=[
            jax.ShapeDtypeStruct((cols, rows), bf16),
            jax.ShapeDtypeStruct((cols, rows), f32),
        ],
        compiler_params=pltpu.CompilerParams(vmem_limit_bytes=VMEM_LIMIT),
        name="finish",
    )(core[None], near, far, x_near, x_far, gradient_t, error_t)


def add_gram(p, g_ref):
    wide = 2 * LANES
    for i in range(0, p.shape[0], wide):
        g_ref[i : i + wide, i:] += dot(p[i : i + wide], p[i:], ((1,), (1,)), None)


def inverse_factor(block, held):
    n = LANES // TILE
    sub = lax.broadcasted_iota(jnp.int32, (TILE, LANES), 0)
    lane = lax.broadcasted_iota(jnp.int32, (TILE, LANES), 1)
    full = lambda v: jnp.broadcast_to(v, (TILE, LANES))
    scale = full(full(block[:TILE, :1])[:1])
    root = lax.rsqrt(scale)
    scale = 1.0 / scale
    panel = [block[TILE * t : TILE * (t + 1)] * scale for t in range(n)]
    out = []
    for t in range(n):
        at = TILE * t
        pivot_lanes = (lane >= at) & (lane < at + TILE)
        column = lambda p: [full(panel[p][:, at + k : at + k + 1]) for k in range(TILE)]
        cols = column(t)
        for k in range(TILE):
            held[k] = cols[k]
        s = [[full(held[k, i : i + 1]) for k in range(i + 1)] for i in range(TILE)]
        later = range(t + 1, n)
        e = {p: column(p) for p in later}
        for p in later:
            panel[p] = jnp.where(pivot_lanes, 0.0, panel[p])
        own = jnp.where(pivot_lanes, jnp.where(lane == sub + at, 1.0, 0.0), panel[t])
        held[TILE] = own
        rows = [full(held[TILE, k : k + 1]) for k in range(TILE)]
        pivots = result = None
        steps = []
        for k in range(0, TILE, 2):
            d0, d1, d2 = s[k][k], s[k + 1][k], s[k + 1][k + 1]
            det = d0 * d2 - d1 * d1
            inv = 1.0 / det
            q = {i: (s[i][k] * d2 - s[i][k + 1] * d1, s[i][k + 1] * d0 - s[i][k] * d1) for i in range(k + 2, TILE)}
            m = {i: (q[i][0] * inv, q[i][1] * inv) for i in q}
            for i in q:
                for c in range(k + 2, i + 1):
                    s[i][c] = s[i][c] - (q[i][0] * s[c][k] + q[i][1] * s[c][k + 1]) * inv
            r0, r1 = rows[k], rows[k + 1]
            v0, v1 = (d2 * r0 - d1 * r1) * inv, (d0 * r1 - d1 * r0) * inv
            steps.append((v0, v1, m))
            for i in q:
                rows[i] = rows[i] - (m[i][0] * r0 + m[i][1] * r1)
            for p in later[:1]:
                e0, e1 = e[p][k], e[p][k + 1]
                panel[p] = panel[p] - (e0 * v0 + e1 * v1)
                for i in q:
                    e[p][i] = e[p][i] - (m[i][0] * e0 + m[i][1] * e1)
            first = 1.0 / d0
            pivots = d0 if k == 0 else jnp.where(sub == k, d0, pivots)
            pivots = jnp.where(sub == k + 1, det * first, pivots)
            result = r0 if k == 0 else jnp.where(sub == k, r0, result)
            result = jnp.where(sub == k + 1, r1 - (d1 * first) * r0, result)
        out.append(jnp.where(lane < at + TILE, result * (lax.rsqrt(pivots) * root), 0.0))
        if t + 2 < n:
            v = [None] * TILE
            for k in reversed(range(0, TILE, 2)):
                v[k], v[k + 1], m = steps[k // 2]
                for i in m:
                    v[k] = v[k] - m[i][0] * v[i]
                    v[k + 1] = v[k + 1] - m[i][1] * v[i]
            for p in later[1:]:
                terms = [e[p][k] * v[k] for k in range(TILE)]
                while len(terms) > 1:
                    terms = [x + y for x, y in zip(terms[::2], terms[1::2])]
                panel[p] = panel[p] - terms[0]
    return out


def factor_kernel(near_hbm, far_hbm, u_ref, inverse_ref, a, near, far, held, sems):
    n_sh, n_chips, depth, width = near_hbm.shape
    rank = n_sh * depth
    near_copy = pltpu.make_async_copy(near_hbm, near, sems.at[0])
    far_copy = pltpu.make_async_copy(far_hbm, far, sems.at[1])
    near_copy.start()
    far_copy.start()
    a[...] = jnp.zeros_like(a)
    near_copy.wait()

    @pl.loop(0, n_chips)
    def _(i):
        add_gram(near[:, i].reshape(rank, width), a)

    far_copy.wait()

    @pl.loop(0, n_chips)
    def _(i):
        add_gram(far[:, i].reshape(rank, width), a)

    step, pair = LANES, 2 * LANES
    rc = ((1,), (0,))

    @pl.loop(0, rank // step)
    def _(j):
        r0 = pl.multiple_of(j * step, step)
        side = pl.multiple_of(lax.rem(j, 2) * step, step)
        for t, panel in enumerate(inverse_factor(a[pl.ds(r0, step), pl.ds(r0, step)], held)):
            inverse_ref[pl.ds(pl.multiple_of(r0 + TILE * t, TILE), TILE), pl.ds(side, step)] = panel
        inverse = inverse_ref[pl.ds(r0, step), pl.ds(side, step)]

        @pl.loop((j + 1) // 2, rank // pair)
        def _(c):
            at = pl.multiple_of(c * pair, pair)
            u_ref[pl.ds(r0, step), pl.ds(at, pair)] = dot(inverse, a[pl.ds(r0, step), pl.ds(at, pair)], rc)

        @pl.when(lax.rem(j, 2) == 0)
        def _():
            r1 = pl.multiple_of((j + 1) * step, step)
            ut = u_ref[pl.ds(r0, step), pl.ds(r1, step)].T
            inverse_ref[pl.ds(r0, step), step:] = jnp.zeros((step, step), f32)

            @pl.loop(j // 2, rank // pair)
            def _(c):
                at = pl.multiple_of(c * pair, pair)
                a[pl.ds(r1, step), pl.ds(at, pair)] -= dot(ut, u_ref[pl.ds(r0, step), pl.ds(at, pair)], rc)

        @pl.when(lax.rem(j, 2) == 1)
        def _():
            p0 = pl.multiple_of((j - 1) * step, pair)
            before = inverse_ref[pl.ds(p0, step), :step]
            cross = dot(u_ref[pl.ds(p0, step), pl.ds(r0, step)], before, ((0,), (0,)))
            inverse_ref[pl.ds(r0, step), :step] = -dot(inverse, cross, rc)

            @pl.loop((j + 1) // 2, rank // pair)
            def _(i):
                r1 = pl.multiple_of(i * pair, pair)
                ut = u_ref[pl.ds(p0, pair), pl.ds(r1, pair)].T

                @pl.loop(i, rank // pair)
                def _(c):
                    at = pl.multiple_of(c * pair, pair)
                    a[pl.ds(r1, pair), pl.ds(at, pair)] -= dot(ut, u_ref[pl.ds(p0, pair), pl.ds(at, pair)], rc)

def factor(near, far):
    rank = near.shape[0] * near.shape[2]
    return pl.pallas_call(
        factor_kernel,
        out_shape=[
            jax.ShapeDtypeStruct((rank, rank), f32),
            jax.ShapeDtypeStruct((rank, 2 * LANES), f32),
        ],
        in_specs=[pl.BlockSpec(memory_space=pl.ANY)] * 2,
        out_specs=[pl.BlockSpec(memory_space=pltpu.VMEM)] * 2,
        scratch_shapes=[
            pltpu.VMEM((rank, rank), f32),
            pltpu.VMEM(near.shape, bf16),
            pltpu.VMEM(far.shape, bf16),
            pltpu.VMEM((TILE + 1, TILE, LANES), f32),
            pltpu.SemaphoreType.DMA((2,)),
        ],
        compiler_params=pltpu.CompilerParams(vmem_limit_bytes=VMEM_LIMIT),
        cost_estimate=pl.CostEstimate(flops=60_000_000_000, bytes_accessed=8 * rank * rank, transcendentals=0),
        name="factor",
    )(near, far)


def solve_kernel(scale, w_ref, u_ref, inverse_ref, x_ref, y, w):
    pair = 2 * LANES
    rank = u_ref.shape[0]
    n = rank // pair
    block = lambda j: slice(j * pair, (j + 1) * pair)
    for j in range(n):
        value = w_ref[:, block(j)]
        if j:
            value = value - dot(y[:, : j * pair], u_ref[: j * pair, block(j)], ((1,), (0,)), HIGH)
        y[:, block(j)] = dot(value, inverse_ref[block(j), :], ((1,), (1,)), HIGH)
    for j in reversed(range(n)):
        value = y[:, block(j)]
        if j < n - 1:
            value = value - dot(w[:, (j + 1) * pair :], u_ref[block(j), (j + 1) * pair :], ((1,), (1,)), HIGH)
        x = dot(value, inverse_ref[block(j), :], ((1,), (0,)), HIGH)
        w[:, block(j)] = x
        x_ref[:, block(j)] = (x * scale).astype(bf16)


def solve(w, u, inverse, scale):
    return pl.pallas_call(
        functools.partial(solve_kernel, scale),
        out_shape=jax.ShapeDtypeStruct(w.shape, bf16),
        in_specs=[pl.BlockSpec(memory_space=pltpu.VMEM)] * 3,
        out_specs=pl.BlockSpec(memory_space=pltpu.VMEM),
        scratch_shapes=[pltpu.VMEM(w.shape, f32)] * 2,
        compiler_params=pltpu.CompilerParams(vmem_limit_bytes=VMEM_LIMIT),
        cost_estimate=pl.CostEstimate(flops=8_000_000_000, bytes_accessed=16 * 2**20, transcendentals=0),
        name="solve",
    )(w, u, inverse)


def shards(gradients, error_memory, q_factor):
    core = lax.axis_index(CORE)
    n_chips = lax.axis_size(CHIPS)
    n_dp = 2 * n_chips
    n_sh = lax.axis_size(SHARD)
    rows, cols = gradients.shape[1:]
    rank = q_factor.shape[1]
    own = -(-rows // (n_dp * LANES)) * LANES
    wide = -(-cols // (n_dp * 16)) * n_dp * 16
    gradient_t, error_t = gradients[0].T, error_memory[0].T

    with jax.named_scope("total"):
        mine, other = cut(core, gradient_t, error_t, n_chips, own)
        got = lax.ppermute(other, CORE, SWAP)
        pair = (mine.astype(f32) + got.astype(f32)).astype(bf16)
        arrived = lax.all_to_all(pair, CHIPS, 0, 0, tiled=True)
        total_t = jnp.sum(arrived.astype(f32), axis=0)

    with jax.named_scope("left"):
        part = dot(q_factor.astype(f32), total_t, ((0,), (0,))).astype(bf16)
        arrived = lax.all_to_all(part.reshape(n_sh, rank // n_sh, own), SHARD, 0, 0, tiled=True)
        p_own = jnp.sum(arrived.astype(f32), axis=0).astype(bf16)
        p_near = spread(p_own, SHARD + CHIPS, n_sh * n_chips).reshape(n_sh, n_chips, rank // n_sh, own)
        p_far = lax.ppermute(p_near, CORE, SWAP)

    with jax.named_scope("right"):
        p_t = lax.dynamic_index_in_dim(p_near, lax.axis_index(CHIPS), 1, keepdims=False).reshape(rank, own)
        total_wide = jnp.pad(total_t, ((0, wide - cols), (0, 0)))
        w_part = dot(total_wide, p_t.astype(f32), ((1,), (1,)), HIGH)
        w_parts = lax.all_to_all(w_part.reshape(n_dp, wide // n_dp, rank), DP, 0, 0, tiled=True)

    with jax.named_scope("solve"):
        u, inverse = factor(p_near, p_far)
        w_parts, inverse = lax.optimization_barrier((w_parts, inverse))
        x_own = solve(jnp.sum(w_parts, axis=0), u, inverse, 1.0 / n_dp)

    with jax.named_scope("rebuild"):
        x_near = spread(x_own, CHIPS, n_chips)
        x_far = lax.ppermute(x_near, CORE, SWAP)
        rebuilt_t, new_error_t = finish(core, p_near, p_far, x_near, x_far, gradient_t, error_t)
    return (rebuilt_t.T, new_error_t.T[None])


def solution(mesh):
    fine = Mesh(mesh.devices.reshape(4, 2, 2, 2, 4), ("x", "yh", "c", "yl", "z"))
    in_specs = (P(DP, None, SHARD), P(DP, None, SHARD), P(SHARD, None))
    out_specs = (P(None, SHARD), P(DP, None, SHARD))
    return jax.shard_map(shards, mesh=fine, in_specs=in_specs, out_specs=out_specs, check_vma=False)
```

```python
import functools

import jax
import jax.numpy as jnp
from jax import lax
from jax.experimental import pallas as pl
from jax.experimental.pallas import tpu as pltpu
from jax.sharding import Mesh, PartitionSpec as P

f32 = jnp.float32
bf16 = jnp.bfloat16
HIGHEST = lax.Precision.HIGHEST
HIGH = lax.Precision.HIGH

CHIPS = ("x", "yh")
CORE = "c"
SHARD = ("yl", "z")
DP = CHIPS + (CORE,)
SWAP = [(0, 1), (1, 0)]

TILE, LANES = 8, 128
MIB = 2**20


def dot(a, b, dims, precision=HIGHEST):
    return lax.dot_general(a, b, (dims, ((), ())), precision=precision, preferred_element_type=f32)


def spread(a, axes, n):
    blocks = jnp.broadcast_to(a[None], (n,) + a.shape)
    return lax.all_to_all(blocks, axes, 0, 0, tiled=True)


def cut_kernel(rows, core_ref, g_ref, e_ref, mine_ref, other_ref):
    core = core_ref[0]
    width = mine_ref.shape[2]
    combined = g_ref[...].astype(f32) + e_ref[...]
    at = pl.program_id(0) * 2 * width + lax.broadcasted_iota(jnp.int32, combined.shape, 1)
    combined = jnp.where(at < rows, combined, 0.0).astype(bf16)
    low, high = combined[:, :width], combined[:, width:]

    @pl.when(core == 0)
    def _():
        mine_ref[0], other_ref[0] = low, high

    @pl.when(core != 0)
    def _():
        mine_ref[0], other_ref[0] = high, low


def cut(core, gradient_t, error_t, n_chips, width):
    cols, rows = gradient_t.shape
    whole = pl.BlockSpec((cols, 2 * width), lambda i, core: (0, i))
    part = pl.BlockSpec((1, cols, width), lambda i, core: (i, 0, 0))
    shape = jax.ShapeDtypeStruct((n_chips, cols, width), bf16)
    return pl.pallas_call(
        functools.partial(cut_kernel, rows),
        grid_spec=pltpu.PrefetchScalarGridSpec(
            num_scalar_prefetch=1, grid=(n_chips,), in_specs=[whole, whole], out_specs=[part, part]
        ),
        out_shape=[shape, shape],
        compiler_params=pltpu.CompilerParams(vmem_limit_bytes=48 * MIB),
        name="cut",
    )(core[None], gradient_t, error_t)


def finish_kernel(core_ref, near_ref, far_ref, x_near_ref, x_far_ref, g_ref, e_ref, rebuilt_ref, error_ref, x):
    core = core_ref[0]
    n_sh, _, depth, width = near_ref.shape
    cols = g_ref.shape[0]
    n_chips, band, _ = x_near_ref.shape

    @pl.when(pl.program_id(0) == 0)
    def _():
        for i in range(n_chips):
            x[pl.ds(pl.multiple_of((2 * i + core) * band, band), band)] = x_near_ref[i]
            x[pl.ds(pl.multiple_of((2 * i + 1 - core) * band, band), band)] = x_far_ref[i]

    def store(columns, ref):
        value = dot(x[:cols], ref[:, 0].reshape(n_sh * depth, width), ((1,), (0,)), None)
        rebuilt_ref[:, columns] = value.astype(bf16)
        error_ref[:, columns] = g_ref[:, columns].astype(f32) + e_ref[:, columns] - value

    low, high = pl.ds(0, width), pl.ds(width, width)

    @pl.when(core == 0)
    def _():
        store(low, near_ref)
        store(high, far_ref)

    @pl.when(core != 0)
    def _():
        store(low, far_ref)
        store(high, near_ref)


def finish(core, near, far, x_near, x_far, gradient_t, error_t):
    cols, rows = gradient_t.shape
    n_sh, n_chips, depth, width = near.shape
    whole = pl.BlockSpec((cols, 2 * width), lambda i, core: (0, i))
    part = pl.BlockSpec((n_sh, 1, depth, width), lambda i, core: (0, i, 0, 0))
    fixed = pl.BlockSpec(x_near.shape, lambda i, core: (0, 0, 0))
    return pl.pallas_call(
        finish_kernel,
        grid_spec=pltpu.PrefetchScalarGridSpec(
            num_scalar_prefetch=1,
            grid=(n_chips,),
            in_specs=[part, part, fixed, fixed, whole, whole],
            out_specs=[whole, whole],
            scratch_shapes=[pltpu.VMEM((n_chips * 2 * x_near.shape[1], x_near.shape[2]), bf16)],
        ),
        out_shape=[
            jax.ShapeDtypeStruct((cols, rows), bf16),
            jax.ShapeDtypeStruct((cols, rows), f32),
        ],
        compiler_params=pltpu.CompilerParams(vmem_limit_bytes=20 * MIB),
        name="finish",
    )(core[None], near, far, x_near, x_far, gradient_t, error_t)


def add_gram(p, g_ref):
    wide = 2 * LANES
    for i in range(0, p.shape[0], wide):
        g_ref[i : i + wide, i:] += dot(p[i : i + wide], p[i:], ((1,), (1,)), None)


def inverse_factor(block, held):
    n = LANES // TILE
    sub = lax.broadcasted_iota(jnp.int32, (TILE, LANES), 0)
    lane = lax.broadcasted_iota(jnp.int32, (TILE, LANES), 1)
    full = lambda v: jnp.broadcast_to(v, (TILE, LANES))
    scale = full(full(block[:TILE, :1])[:1])
    root = lax.rsqrt(scale)
    scale = 1.0 / scale
    panel = [block[TILE * t : TILE * (t + 1)] * scale for t in range(n)]
    out = []
    for t in range(n):
        at = TILE * t
        pivot_lanes = (lane >= at) & (lane < at + TILE)
        column = lambda p: [full(panel[p][:, at + k : at + k + 1]) for k in range(TILE)]
        cols = column(t)
        for k in range(TILE):
            held[k] = cols[k]
        s = [[full(held[k, i : i + 1]) for k in range(i + 1)] for i in range(TILE)]
        later = range(t + 1, n)
        e = {p: column(p) for p in later}
        for p in later:
            panel[p] = jnp.where(pivot_lanes, 0.0, panel[p])
        own = jnp.where(pivot_lanes, jnp.where(lane == sub + at, 1.0, 0.0), panel[t])
        held[TILE] = own
        rows = [full(held[TILE, k : k + 1]) for k in range(TILE)]
        pivots = result = None
        steps = []
        for k in range(0, TILE, 2):
            d0, d1, d2 = s[k][k], s[k + 1][k], s[k + 1][k + 1]
            det = d0 * d2 - d1 * d1
            inv = 1.0 / det
            q = {i: (s[i][k] * d2 - s[i][k + 1] * d1, s[i][k + 1] * d0 - s[i][k] * d1) for i in range(k + 2, TILE)}
            m = {i: (q[i][0] * inv, q[i][1] * inv) for i in q}
            for i in q:
                for c in range(k + 2, i + 1):
                    s[i][c] = s[i][c] - (q[i][0] * s[c][k] + q[i][1] * s[c][k + 1]) * inv
            r0, r1 = rows[k], rows[k + 1]
            v0, v1 = (d2 * r0 - d1 * r1) * inv, (d0 * r1 - d1 * r0) * inv
            steps.append((v0, v1, m))
            for i in q:
                rows[i] = rows[i] - (m[i][0] * r0 + m[i][1] * r1)
            for p in later[:1]:
                e0, e1 = e[p][k], e[p][k + 1]
                panel[p] = panel[p] - (e0 * v0 + e1 * v1)
                for i in q:
                    e[p][i] = e[p][i] - (m[i][0] * e0 + m[i][1] * e1)
            first = 1.0 / d0
            pivots = d0 if k == 0 else jnp.where(sub == k, d0, pivots)
            pivots = jnp.where(sub == k + 1, det * first, pivots)
            result = r0 if k == 0 else jnp.where(sub == k, r0, result)
            result = jnp.where(sub == k + 1, r1 - (d1 * first) * r0, result)
        out.append(jnp.where(lane < at + TILE, result * (lax.rsqrt(pivots) * root), 0.0))
        if t + 2 < n:
            v = [None] * TILE
            for k in reversed(range(0, TILE, 2)):
                v[k], v[k + 1], m = steps[k // 2]
                for i in m:
                    v[k] = v[k] - m[i][0] * v[i]
                    v[k + 1] = v[k + 1] - m[i][1] * v[i]
            for p in later[1:]:
                terms = [e[p][k] * v[k] for k in range(TILE)]
                while len(terms) > 1:
                    terms = [x + y for x, y in zip(terms[::2], terms[1::2])]
                panel[p] = panel[p] - terms[0]
    return out


def factor_kernel(near_hbm, far_hbm, u_ref, inverse_ref, a, near, far, held, sems):
    n_sh, n_chips, depth, width = near_hbm.shape
    rank = n_sh * depth
    near_copy = pltpu.make_async_copy(near_hbm, near, sems.at[0])
    far_copy = pltpu.make_async_copy(far_hbm, far, sems.at[1])
    near_copy.start()
    far_copy.start()
    a[...] = jnp.zeros_like(a)
    near_copy.wait()

    @pl.loop(0, n_chips)
    def _(i):
        add_gram(near[:, i].reshape(rank, width), a)

    far_copy.wait()

    @pl.loop(0, n_chips)
    def _(i):
        add_gram(far[:, i].reshape(rank, width), a)

    step, pair = LANES, 2 * LANES
    rc = ((1,), (0,))

    @pl.loop(0, rank // step)
    def _(j):
        r0 = pl.multiple_of(j * step, step)
        side = pl.multiple_of(lax.rem(j, 2) * step, step)
        for t, panel in enumerate(inverse_factor(a[pl.ds(r0, step), pl.ds(r0, step)], held)):
            inverse_ref[pl.ds(pl.multiple_of(r0 + TILE * t, TILE), TILE), pl.ds(side, step)] = panel
        inverse = inverse_ref[pl.ds(r0, step), pl.ds(side, step)]

        @pl.loop((j + 1) // 2, rank // pair)
        def _(c):
            at = pl.multiple_of(c * pair, pair)
            u_ref[pl.ds(r0, step), pl.ds(at, pair)] = dot(inverse, a[pl.ds(r0, step), pl.ds(at, pair)], rc)

        @pl.when(lax.rem(j, 2) == 0)
        def _():
            r1 = pl.multiple_of((j + 1) * step, step)
            ut = u_ref[pl.ds(r0, step), pl.ds(r1, step)].T
            inverse_ref[pl.ds(r0, step), step:] = jnp.zeros((step, step), f32)

            @pl.loop(j // 2, rank // pair)
            def _(c):
                at = pl.multiple_of(c * pair, pair)
                a[pl.ds(r1, step), pl.ds(at, pair)] -= dot(ut, u_ref[pl.ds(r0, step), pl.ds(at, pair)], rc)

        @pl.when(lax.rem(j, 2) == 1)
        def _():
            p0 = pl.multiple_of((j - 1) * step, pair)
            before = inverse_ref[pl.ds(p0, step), :step]
            cross = dot(u_ref[pl.ds(p0, step), pl.ds(r0, step)], before, ((0,), (0,)))
            inverse_ref[pl.ds(r0, step), :step] = -dot(inverse, cross, rc)

            @pl.loop((j + 1) // 2, rank // pair)
            def _(i):
                r1 = pl.multiple_of(i * pair, pair)
                ut = u_ref[pl.ds(p0, pair), pl.ds(r1, pair)].T

                @pl.loop(i, rank // pair)
                def _(c):
                    at = pl.multiple_of(c * pair, pair)
                    a[pl.ds(r1, pair), pl.ds(at, pair)] -= dot(ut, u_ref[pl.ds(p0, pair), pl.ds(at, pair)], rc)

def factor(near, far):
    rank = near.shape[0] * near.shape[2]
    return pl.pallas_call(
        factor_kernel,
        out_shape=[
            jax.ShapeDtypeStruct((rank, rank), f32),
            jax.ShapeDtypeStruct((rank, 2 * LANES), f32),
        ],
        in_specs=[pl.BlockSpec(memory_space=pl.ANY)] * 2,
        out_specs=[pl.BlockSpec(memory_space=pltpu.VMEM)] * 2,
        scratch_shapes=[
            pltpu.VMEM((rank, rank), f32),
            pltpu.VMEM(near.shape, bf16),
            pltpu.VMEM(far.shape, bf16),
            pltpu.VMEM((TILE + 1, TILE, LANES), f32),
            pltpu.SemaphoreType.DMA((2,)),
        ],
        compiler_params=pltpu.CompilerParams(vmem_limit_bytes=28 * MIB),
        cost_estimate=pl.CostEstimate(flops=60_000_000_000, bytes_accessed=8 * rank * rank, transcendentals=0),
        name="factor",
    )(near, far)


def solve_kernel(scale, w_ref, u_ref, inverse_ref, x_ref, y, w):
    pair = 2 * LANES
    rank = u_ref.shape[0]
    n = rank // pair
    block = lambda j: slice(j * pair, (j + 1) * pair)
    for j in range(n):
        value = w_ref[:, block(j)]
        if j:
            value = value - dot(y[:, : j * pair], u_ref[: j * pair, block(j)], ((1,), (0,)), HIGH)
        y[:, block(j)] = dot(value, inverse_ref[block(j), :], ((1,), (1,)), HIGH)
    for j in reversed(range(n)):
        value = y[:, block(j)]
        if j < n - 1:
            value = value - dot(w[:, (j + 1) * pair :], u_ref[block(j), (j + 1) * pair :], ((1,), (1,)), HIGH)
        x = dot(value, inverse_ref[block(j), :], ((1,), (0,)), HIGH)
        w[:, block(j)] = x
        x_ref[:, block(j)] = (x * scale).astype(bf16)


def solve(w, u, inverse, scale):
    return pl.pallas_call(
        functools.partial(solve_kernel, scale),
        out_shape=jax.ShapeDtypeStruct(w.shape, bf16),
        in_specs=[pl.BlockSpec(memory_space=pltpu.VMEM)] * 3,
        out_specs=pl.BlockSpec(memory_space=pltpu.VMEM),
        scratch_shapes=[pltpu.VMEM(w.shape, f32)] * 2,
        compiler_params=pltpu.CompilerParams(vmem_limit_bytes=16 * MIB),
        cost_estimate=pl.CostEstimate(flops=8_000_000_000, bytes_accessed=16 * 2**20, transcendentals=0),
        name="solve",
    )(w, u, inverse)


def shards(gradients, error_memory, q_factor):
    core = lax.axis_index(CORE)
    n_chips = lax.axis_size(CHIPS)
    n_dp = 2 * n_chips
    n_sh = lax.axis_size(SHARD)
    rows, cols = gradients.shape[1:]
    rank = q_factor.shape[1]
    own = -(-rows // (n_dp * LANES)) * LANES
    wide = -(-cols // (n_dp * 16)) * n_dp * 16
    gradient_t, error_t = gradients[0].T, error_memory[0].T

    with jax.named_scope("total"):
        mine, other = cut(core, gradient_t, error_t, n_chips, own)
        got = lax.ppermute(other, CORE, SWAP)
        pair = (mine.astype(f32) + got.astype(f32)).astype(bf16)
        arrived = lax.all_to_all(pair, CHIPS, 0, 0, tiled=True)
        total_t = jnp.sum(arrived.astype(f32), axis=0)

    with jax.named_scope("left"):
        part = dot(q_factor.astype(f32), total_t, ((0,), (0,))).astype(bf16)
        arrived = lax.all_to_all(part.reshape(n_sh, rank // n_sh, own), SHARD, 0, 0, tiled=True)
        p_own = jnp.sum(arrived.astype(f32), axis=0).astype(bf16)
        p_near = spread(p_own, SHARD + CHIPS, n_sh * n_chips).reshape(n_sh, n_chips, rank // n_sh, own)
        p_far = lax.ppermute(p_near, CORE, SWAP)

    with jax.named_scope("right"):
        p_t = lax.dynamic_index_in_dim(p_near, lax.axis_index(CHIPS), 1, keepdims=False).reshape(rank, own)
        total_wide = jnp.pad(total_t, ((0, wide - cols), (0, 0)))
        w_part = dot(total_wide, p_t.astype(f32), ((1,), (1,)), HIGH)
        w_parts = lax.all_to_all(w_part.reshape(n_dp, wide // n_dp, rank), DP, 0, 0, tiled=True)

    with jax.named_scope("solve"):
        u, inverse = factor(p_near, p_far)
        w_parts, inverse = lax.optimization_barrier((w_parts, inverse))
        x_own = solve(jnp.sum(w_parts, axis=0), u, inverse, 1.0 / n_dp)

    with jax.named_scope("rebuild"):
        x_near = spread(x_own, CHIPS, n_chips)
        x_far = lax.ppermute(x_near, CORE, SWAP)
        rebuilt_t, new_error_t = finish(core, p_near, p_far, x_near, x_far, gradient_t, error_t)
    return (rebuilt_t.T, new_error_t.T[None])


def solution(mesh):
    fine = Mesh(mesh.devices.reshape(4, 2, 2, 2, 4), ("x", "yh", "c", "yl", "z"))
    in_specs = (P(DP, None, SHARD), P(DP, None, SHARD), P(SHARD, None))
    out_specs = (P(None, SHARD), P(DP, None, SHARD))
    return jax.shard_map(shards, mesh=fine, in_specs=in_specs, out_specs=out_specs, check_vma=False)
```

```python
import functools

import jax
import jax.numpy as jnp
from jax import lax
from jax.experimental import pallas as pl
from jax.experimental.pallas import tpu as pltpu
from jax.sharding import Mesh, PartitionSpec as P

f32 = jnp.float32
bf16 = jnp.bfloat16
HIGHEST = lax.Precision.HIGHEST
HIGH = lax.Precision.HIGH

CHIPS = ("x", "yh")
CORE = "c"
SHARD = ("yl", "z")
DP = CHIPS + (CORE,)
SWAP = [(0, 1), (1, 0)]

TILE, LANES = 8, 128
MIB = 2**20


def dot(a, b, dims, precision=HIGHEST):
    return lax.dot_general(a, b, (dims, ((), ())), precision=precision, preferred_element_type=f32)


def spread(a, axes, n):
    blocks = jnp.broadcast_to(a[None], (n,) + a.shape)
    return lax.all_to_all(blocks, axes, 0, 0, tiled=True)


def cut_kernel(rows, core_ref, g_ref, e_ref, mine_ref, other_ref):
    core = core_ref[0]
    width = mine_ref.shape[2]
    combined = g_ref[...].astype(f32) + e_ref[...]
    at = pl.program_id(0) * 2 * width + lax.broadcasted_iota(jnp.int32, combined.shape, 1)
    combined = jnp.where(at < rows, combined, 0.0).astype(bf16)
    low, high = combined[:, :width], combined[:, width:]

    @pl.when(core == 0)
    def _():
        mine_ref[0], other_ref[0] = low, high

    @pl.when(core != 0)
    def _():
        mine_ref[0], other_ref[0] = high, low


def cut(core, gradient_t, error_t, n_chips, width):
    cols, rows = gradient_t.shape
    whole = pl.BlockSpec((cols, 2 * width), lambda i, core: (0, i))
    part = pl.BlockSpec((1, cols, width), lambda i, core: (i, 0, 0))
    shape = jax.ShapeDtypeStruct((n_chips, cols, width), bf16)
    return pl.pallas_call(
        functools.partial(cut_kernel, rows),
        grid_spec=pltpu.PrefetchScalarGridSpec(
            num_scalar_prefetch=1, grid=(n_chips,), in_specs=[whole, whole], out_specs=[part, part]
        ),
        out_shape=[shape, shape],
        compiler_params=pltpu.CompilerParams(vmem_limit_bytes=48 * MIB),
        name="cut",
    )(core[None], gradient_t, error_t)


def finish_kernel(core_ref, near_ref, far_ref, x_near_ref, x_far_ref, g_ref, e_ref, rebuilt_ref, error_ref, x):
    core = core_ref[0]
    n_sh, _, depth, width = near_ref.shape
    cols = g_ref.shape[0]
    n_chips, band, _ = x_near_ref.shape

    @pl.when(pl.program_id(0) == 0)
    def _():
        for i in range(n_chips):
            x[pl.ds(pl.multiple_of((2 * i + core) * band, band), band)] = x_near_ref[i]
            x[pl.ds(pl.multiple_of((2 * i + 1 - core) * band, band), band)] = x_far_ref[i]

    def store(columns, ref):
        value = dot(x[:cols], ref[:, 0].reshape(n_sh * depth, width), ((1,), (0,)), None)
        rebuilt_ref[:, columns] = value.astype(bf16)
        error_ref[:, columns] = g_ref[:, columns].astype(f32) + e_ref[:, columns] - value

    low, high = pl.ds(0, width), pl.ds(width, width)

    @pl.when(core == 0)
    def _():
        store(low, near_ref)
        store(high, far_ref)

    @pl.when(core != 0)
    def _():
        store(low, far_ref)
        store(high, near_ref)


def finish(core, near, far, x_near, x_far, gradient_t, error_t):
    cols, rows = gradient_t.shape
    n_sh, n_chips, depth, width = near.shape
    whole = pl.BlockSpec((cols, 2 * width), lambda i, core: (0, i))
    part = pl.BlockSpec((n_sh, 1, depth, width), lambda i, core: (0, i, 0, 0))
    fixed = pl.BlockSpec(x_near.shape, lambda i, core: (0, 0, 0))
    return pl.pallas_call(
        finish_kernel,
        grid_spec=pltpu.PrefetchScalarGridSpec(
            num_scalar_prefetch=1,
            grid=(n_chips,),
            in_specs=[part, part, fixed, fixed, whole, whole],
            out_specs=[whole, whole],
            scratch_shapes=[pltpu.VMEM((n_chips * 2 * x_near.shape[1], x_near.shape[2]), bf16)],
        ),
        out_shape=[
            jax.ShapeDtypeStruct((cols, rows), bf16),
            jax.ShapeDtypeStruct((cols, rows), f32),
        ],
        compiler_params=pltpu.CompilerParams(vmem_limit_bytes=20 * MIB),
        name="finish",
    )(core[None], near, far, x_near, x_far, gradient_t, error_t)


def add_gram(p, g_ref):
    wide = 2 * LANES
    for i in range(0, p.shape[0], wide):
        g_ref[i : i + wide, i:] += dot(p[i : i + wide], p[i:], ((1,), (1,)), None)


def inverse_factor(block, held):
    n = LANES // TILE
    sub = lax.broadcasted_iota(jnp.int32, (TILE, LANES), 0)
    lane = lax.broadcasted_iota(jnp.int32, (TILE, LANES), 1)
    full = lambda v: jnp.broadcast_to(v, (TILE, LANES))
    scale = full(full(block[:TILE, :1])[:1])
    root = lax.rsqrt(scale)
    scale = 1.0 / scale
    panel = [block[TILE * t : TILE * (t + 1)] * scale for t in range(n)]
    out = []
    for t in range(n):
        at = TILE * t
        pivot_lanes = (lane >= at) & (lane < at + TILE)
        column = lambda p: [full(panel[p][:, at + k : at + k + 1]) for k in range(TILE)]
        cols = column(t)
        for k in range(TILE):
            held[k] = cols[k]
        s = [[full(held[k, i : i + 1]) for k in range(i + 1)] for i in range(TILE)]
        later = range(t + 1, n)
        e = {p: column(p) for p in later}
        for p in later:
            panel[p] = jnp.where(pivot_lanes, 0.0, panel[p])
        own = jnp.where(pivot_lanes, jnp.where(lane == sub + at, 1.0, 0.0), panel[t])
        held[TILE] = own
        rows = [full(held[TILE, k : k + 1]) for k in range(TILE)]
        pivots = result = None
        steps = []
        for k in range(0, TILE, 2):
            d0, d1, d2 = s[k][k], s[k + 1][k], s[k + 1][k + 1]
            det = d0 * d2 - d1 * d1
            inv = 1.0 / det
            q = {i: (s[i][k] * d2 - s[i][k + 1] * d1, s[i][k + 1] * d0 - s[i][k] * d1) for i in range(k + 2, TILE)}
            m = {i: (q[i][0] * inv, q[i][1] * inv) for i in q}
            for i in q:
                for c in range(k + 2, i + 1):
                    s[i][c] = s[i][c] - (q[i][0] * s[c][k] + q[i][1] * s[c][k + 1]) * inv
            r0, r1 = rows[k], rows[k + 1]
            v0, v1 = (d2 * r0 - d1 * r1) * inv, (d0 * r1 - d1 * r0) * inv
            steps.append((v0, v1, m))
            for i in q:
                rows[i] = rows[i] - (m[i][0] * r0 + m[i][1] * r1)
            for p in later[:1]:
                e0, e1 = e[p][k], e[p][k + 1]
                panel[p] = panel[p] - (e0 * v0 + e1 * v1)
                for i in q:
                    e[p][i] = e[p][i] - (m[i][0] * e0 + m[i][1] * e1)
            first = 1.0 / d0
            pivots = d0 if k == 0 else jnp.where(sub == k, d0, pivots)
            pivots = jnp.where(sub == k + 1, det * first, pivots)
            result = r0 if k == 0 else jnp.where(sub == k, r0, result)
            result = jnp.where(sub == k + 1, r1 - (d1 * first) * r0, result)
        out.append(jnp.where(lane < at + TILE, result * (lax.rsqrt(pivots) * root), 0.0))
        if t + 2 < n:
            v = [None] * TILE
            for k in reversed(range(0, TILE, 2)):
                v[k], v[k + 1], m = steps[k // 2]
                for i in m:
                    v[k] = v[k] - m[i][0] * v[i]
                    v[k + 1] = v[k + 1] - m[i][1] * v[i]
            for p in later[1:]:
                terms = [e[p][k] * v[k] for k in range(TILE)]
                while len(terms) > 1:
                    terms = [x + y for x, y in zip(terms[::2], terms[1::2])]
                panel[p] = panel[p] - terms[0]
    return out


def packing(rank, pair):
    at, out = 0, []
    for i in range(rank // pair - 1):
        size = rank - (i + 1) * pair
        out.append((i, at, size))
        at += size
    return out


def factor_kernel(near_hbm, far_hbm, packed_ref, inverse_ref, a, u_ref, near, far, held, sems):
    n_sh, n_chips, depth, width = near_hbm.shape
    rank = n_sh * depth
    near_copy = pltpu.make_async_copy(near_hbm, near, sems.at[0])
    far_copy = pltpu.make_async_copy(far_hbm, far, sems.at[1])
    near_copy.start()
    far_copy.start()
    a[...] = jnp.zeros_like(a)
    near_copy.wait()

    @pl.loop(0, n_chips)
    def _(i):
        add_gram(near[:, i].reshape(rank, width), a)

    far_copy.wait()

    @pl.loop(0, n_chips)
    def _(i):
        add_gram(far[:, i].reshape(rank, width), a)

    step, pair = LANES, 2 * LANES
    rc = ((1,), (0,))

    @pl.loop(0, rank // step)
    def _(j):
        r0 = pl.multiple_of(j * step, step)
        side = pl.multiple_of(lax.rem(j, 2) * step, step)
        for t, panel in enumerate(inverse_factor(a[pl.ds(r0, step), pl.ds(r0, step)], held)):
            inverse_ref[pl.ds(pl.multiple_of(r0 + TILE * t, TILE), TILE), pl.ds(side, step)] = panel
        inverse = inverse_ref[pl.ds(r0, step), pl.ds(side, step)]

        @pl.loop((j + 1) // 2, rank // pair)
        def _(c):
            at = pl.multiple_of(c * pair, pair)
            u_ref[pl.ds(r0, step), pl.ds(at, pair)] = dot(inverse, a[pl.ds(r0, step), pl.ds(at, pair)], rc)

        @pl.when(lax.rem(j, 2) == 0)
        def _():
            r1 = pl.multiple_of((j + 1) * step, step)
            ut = u_ref[pl.ds(r0, step), pl.ds(r1, step)].T
            inverse_ref[pl.ds(r0, step), step:] = jnp.zeros((step, step), f32)

            @pl.loop(j // 2, rank // pair)
            def _(c):
                at = pl.multiple_of(c * pair, pair)
                a[pl.ds(r1, step), pl.ds(at, pair)] -= dot(ut, u_ref[pl.ds(r0, step), pl.ds(at, pair)], rc)

        @pl.when(lax.rem(j, 2) == 1)
        def _():
            p0 = pl.multiple_of((j - 1) * step, pair)
            before = inverse_ref[pl.ds(p0, step), :step]
            cross = dot(u_ref[pl.ds(p0, step), pl.ds(r0, step)], before, ((0,), (0,)))
            inverse_ref[pl.ds(r0, step), :step] = -dot(inverse, cross, rc)

            @pl.loop((j + 1) // 2, rank // pair)
            def _(i):
                r1 = pl.multiple_of(i * pair, pair)
                ut = u_ref[pl.ds(p0, pair), pl.ds(r1, pair)].T

                @pl.loop(i, rank // pair)
                def _(c):
                    at = pl.multiple_of(c * pair, pair)
                    a[pl.ds(r1, pair), pl.ds(at, pair)] -= dot(ut, u_ref[pl.ds(p0, pair), pl.ds(at, pair)], rc)
    for i, at, size in packing(rank, pair):
        packed_ref[:, at : at + size] = u_ref[i * pair : (i + 1) * pair, rank - size :]


def factor(near, far):
    rank = near.shape[0] * near.shape[2]
    return pl.pallas_call(
        factor_kernel,
        out_shape=[
            jax.ShapeDtypeStruct((2 * LANES, sum(size for _, _, size in packing(rank, 2 * LANES))), f32),
            jax.ShapeDtypeStruct((rank, 2 * LANES), f32),
        ],
        in_specs=[pl.BlockSpec(memory_space=pl.ANY)] * 2,
        out_specs=[pl.BlockSpec(memory_space=pltpu.VMEM)] * 2,
        scratch_shapes=[
            pltpu.VMEM((rank, rank), f32),
            pltpu.VMEM((rank, rank), f32),
            pltpu.VMEM(near.shape, bf16),
            pltpu.VMEM(far.shape, bf16),
            pltpu.VMEM((TILE + 1, TILE, LANES), f32),
            pltpu.SemaphoreType.DMA((2,)),
        ],
        compiler_params=pltpu.CompilerParams(vmem_limit_bytes=28 * MIB),
        cost_estimate=pl.CostEstimate(flops=60_000_000_000, bytes_accessed=8 * rank * rank, transcendentals=0),
        name="factor",
    )(near, far)


def solve_kernel(scale, w_ref, u_ref, inverse_ref, x_ref, y, w):
    pair = 2 * LANES
    rank = w_ref.shape[1]
    n = rank // pair
    start = {i: at for i, at, _ in packing(rank, pair)}
    block = lambda j: slice(j * pair, (j + 1) * pair)
    for j in range(n):
        value = w_ref[:, block(j)]
        for i in range(j):
            at = start[i] + (j - i - 1) * pair
            value = value - dot(y[:, block(i)], u_ref[:, at : at + pair], ((1,), (0,)), HIGH)
        y[:, block(j)] = dot(value, inverse_ref[block(j), :], ((1,), (1,)), HIGH)
    for j in reversed(range(n)):
        value = y[:, block(j)]
        if j < n - 1:
            value = value - dot(
                w[:, (j + 1) * pair :], u_ref[:, start[j] : start[j] + rank - (j + 1) * pair], ((1,), (1,)), HIGH
            )
        x = dot(value, inverse_ref[block(j), :], ((1,), (0,)), HIGH)
        w[:, block(j)] = x
        x_ref[:, block(j)] = (x * scale).astype(bf16)


def solve(w, u, inverse, scale):
    return pl.pallas_call(
        functools.partial(solve_kernel, scale),
        out_shape=jax.ShapeDtypeStruct(w.shape, bf16),
        in_specs=[pl.BlockSpec(memory_space=pltpu.VMEM)] * 3,
        out_specs=pl.BlockSpec(memory_space=pltpu.VMEM),
        scratch_shapes=[pltpu.VMEM(w.shape, f32)] * 2,
        compiler_params=pltpu.CompilerParams(vmem_limit_bytes=16 * MIB),
        cost_estimate=pl.CostEstimate(flops=8_000_000_000, bytes_accessed=16 * 2**20, transcendentals=0),
        name="solve",
    )(w, u, inverse)


def shards(gradients, error_memory, q_factor):
    core = lax.axis_index(CORE)
    n_chips = lax.axis_size(CHIPS)
    n_dp = 2 * n_chips
    n_sh = lax.axis_size(SHARD)
    rows, cols = gradients.shape[1:]
    rank = q_factor.shape[1]
    own = -(-rows // (n_dp * LANES)) * LANES
    wide = -(-cols // (n_dp * 16)) * n_dp * 16
    gradient_t, error_t = gradients[0].T, error_memory[0].T

    with jax.named_scope("total"):
        mine, other = cut(core, gradient_t, error_t, n_chips, own)
        got = lax.ppermute(other, CORE, SWAP)
        pair = (mine.astype(f32) + got.astype(f32)).astype(bf16)
        arrived = lax.all_to_all(pair, CHIPS, 0, 0, tiled=True)
        total_t = jnp.sum(arrived.astype(f32), axis=0)

    with jax.named_scope("left"):
        part = dot(q_factor.astype(f32), total_t, ((0,), (0,))).astype(bf16)
        arrived = lax.all_to_all(part.reshape(n_sh, rank // n_sh, own), SHARD, 0, 0, tiled=True)
        p_own = jnp.sum(arrived.astype(f32), axis=0).astype(bf16)
        p_near = spread(p_own, SHARD + CHIPS, n_sh * n_chips).reshape(n_sh, n_chips, rank // n_sh, own)
        p_far = lax.ppermute(p_near, CORE, SWAP)

    with jax.named_scope("right"):
        p_t = lax.dynamic_index_in_dim(p_near, lax.axis_index(CHIPS), 1, keepdims=False).reshape(rank, own)
        total_wide = jnp.pad(total_t, ((0, wide - cols), (0, 0)))
        w_part = dot(total_wide, p_t.astype(f32), ((1,), (1,)), HIGH)
        w_parts = lax.all_to_all(w_part.reshape(n_dp, wide // n_dp, rank), DP, 0, 0, tiled=True)

    with jax.named_scope("solve"):
        u, inverse = factor(p_near, p_far)
        w_parts, inverse = lax.optimization_barrier((w_parts, inverse))
        x_own = solve(jnp.sum(w_parts, axis=0), u, inverse, 1.0 / n_dp)

    with jax.named_scope("rebuild"):
        x_near = spread(x_own, CHIPS, n_chips)
        x_far = lax.ppermute(x_near, CORE, SWAP)
        rebuilt_t, new_error_t = finish(core, p_near, p_far, x_near, x_far, gradient_t, error_t)
    return (rebuilt_t.T, new_error_t.T[None])


def solution(mesh):
    fine = Mesh(mesh.devices.reshape(4, 2, 2, 2, 4), ("x", "yh", "c", "yl", "z"))
    in_specs = (P(DP, None, SHARD), P(DP, None, SHARD), P(SHARD, None))
    out_specs = (P(None, SHARD), P(DP, None, SHARD))
    return jax.shard_map(shards, mesh=fine, in_specs=in_specs, out_specs=out_specs, check_vma=False)
```

```python
import functools

import jax
import jax.numpy as jnp
from jax import lax
from jax.experimental import pallas as pl
from jax.experimental.pallas import tpu as pltpu
from jax.sharding import Mesh, PartitionSpec as P

f32 = jnp.float32
bf16 = jnp.bfloat16
HIGHEST = lax.Precision.HIGHEST
HIGH = lax.Precision.HIGH

CHIPS = ("x", "yh")
CORE = "c"
SHARD = ("yl", "z")
DP = CHIPS + (CORE,)
SWAP = [(0, 1), (1, 0)]

TILE, LANES = 8, 128
MIB = 2**20


def dot(a, b, dims, precision=HIGHEST):
    return lax.dot_general(a, b, (dims, ((), ())), precision=precision, preferred_element_type=f32)


def spread(a, axes, n):
    blocks = jnp.broadcast_to(a[None], (n,) + a.shape)
    return lax.all_to_all(blocks, axes, 0, 0, tiled=True)


def cut_kernel(rows, core_ref, g_ref, e_ref, mine_ref, other_ref):
    core = core_ref[0]
    width = mine_ref.shape[2]
    combined = g_ref[...].astype(f32) + e_ref[...]
    at = pl.program_id(0) * 2 * width + lax.broadcasted_iota(jnp.int32, combined.shape, 1)
    combined = jnp.where(at < rows, combined, 0.0).astype(bf16)
    low, high = combined[:, :width], combined[:, width:]

    @pl.when(core == 0)
    def _():
        mine_ref[0], other_ref[0] = low, high

    @pl.when(core != 0)
    def _():
        mine_ref[0], other_ref[0] = high, low


def cut(core, gradient_t, error_t, n_chips, width):
    cols, rows = gradient_t.shape
    whole = pl.BlockSpec((cols, 2 * width), lambda i, core: (0, i))
    part = pl.BlockSpec((1, cols, width), lambda i, core: (i, 0, 0))
    shape = jax.ShapeDtypeStruct((n_chips, cols, width), bf16)
    return pl.pallas_call(
        functools.partial(cut_kernel, rows),
        grid_spec=pltpu.PrefetchScalarGridSpec(
            num_scalar_prefetch=1, grid=(n_chips,), in_specs=[whole, whole], out_specs=[part, part]
        ),
        out_shape=[shape, shape],
        compiler_params=pltpu.CompilerParams(vmem_limit_bytes=48 * MIB),
        name="cut",
    )(core[None], gradient_t, error_t)


def finish_kernel(core_ref, near_ref, far_ref, x_near_ref, x_far_ref, g_ref, e_ref, rebuilt_ref, error_ref, x):
    core = core_ref[0]
    n_sh, _, depth, width = near_ref.shape
    cols = g_ref.shape[0]
    n_chips, band, _ = x_near_ref.shape

    @pl.when(pl.program_id(0) == 0)
    def _():
        for i in range(n_chips):
            x[pl.ds(pl.multiple_of((2 * i + core) * band, band), band)] = x_near_ref[i]
            x[pl.ds(pl.multiple_of((2 * i + 1 - core) * band, band), band)] = x_far_ref[i]

    def store(columns, ref):
        value = dot(x[:cols], ref[:, 0].reshape(n_sh * depth, width), ((1,), (0,)), None)
        rebuilt_ref[:, columns] = value.astype(bf16)
        error_ref[:, columns] = g_ref[:, columns].astype(f32) + e_ref[:, columns] - value

    low, high = pl.ds(0, width), pl.ds(width, width)

    @pl.when(core == 0)
    def _():
        store(low, near_ref)
        store(high, far_ref)

    @pl.when(core != 0)
    def _():
        store(low, far_ref)
        store(high, near_ref)


def finish(core, near, far, x_near, x_far, gradient_t, error_t):
    cols, rows = gradient_t.shape
    n_sh, n_chips, depth, width = near.shape
    whole = pl.BlockSpec((cols, 2 * width), lambda i, core: (0, i))
    part = pl.BlockSpec((n_sh, 1, depth, width), lambda i, core: (0, i, 0, 0))
    fixed = pl.BlockSpec(x_near.shape, lambda i, core: (0, 0, 0))
    return pl.pallas_call(
        finish_kernel,
        grid_spec=pltpu.PrefetchScalarGridSpec(
            num_scalar_prefetch=1,
            grid=(n_chips,),
            in_specs=[part, part, fixed, fixed, whole, whole],
            out_specs=[whole, whole],
            scratch_shapes=[pltpu.VMEM((n_chips * 2 * x_near.shape[1], x_near.shape[2]), bf16)],
        ),
        out_shape=[
            jax.ShapeDtypeStruct((cols, rows), bf16),
            jax.ShapeDtypeStruct((cols, rows), f32),
        ],
        compiler_params=pltpu.CompilerParams(vmem_limit_bytes=20 * MIB),
        name="finish",
    )(core[None], near, far, x_near, x_far, gradient_t, error_t)


def add_gram(p, g_ref):
    wide = 2 * LANES
    for i in range(0, p.shape[0], wide):
        g_ref[i : i + wide, i:] += dot(p[i : i + wide], p[i:], ((1,), (1,)), None)


def inverse_factor(block, held):
    n = LANES // TILE
    sub = lax.broadcasted_iota(jnp.int32, (TILE, LANES), 0)
    lane = lax.broadcasted_iota(jnp.int32, (TILE, LANES), 1)
    full = lambda v: jnp.broadcast_to(v, (TILE, LANES))
    scale = full(full(block[:TILE, :1])[:1])
    root = lax.rsqrt(scale)
    scale = 1.0 / scale
    panel = [block[TILE * t : TILE * (t + 1)] * scale for t in range(n)]
    out = []
    for t in range(n):
        at = TILE * t
        pivot_lanes = (lane >= at) & (lane < at + TILE)
        column = lambda p: [full(panel[p][:, at + k : at + k + 1]) for k in range(TILE)]
        cols = column(t)
        for k in range(TILE):
            held[k] = cols[k]
        s = [[full(held[k, i : i + 1]) for k in range(i + 1)] for i in range(TILE)]
        later = range(t + 1, n)
        e = {p: column(p) for p in later}
        for p in later:
            panel[p] = jnp.where(pivot_lanes, 0.0, panel[p])
        own = jnp.where(pivot_lanes, jnp.where(lane == sub + at, 1.0, 0.0), panel[t])
        held[TILE] = own
        rows = [full(held[TILE, k : k + 1]) for k in range(TILE)]
        pivots = result = None
        steps = []
        for k in range(0, TILE, 2):
            d0, d1, d2 = s[k][k], s[k + 1][k], s[k + 1][k + 1]
            det = d0 * d2 - d1 * d1
            inv = 1.0 / det
            q = {i: (s[i][k] * d2 - s[i][k + 1] * d1, s[i][k + 1] * d0 - s[i][k] * d1) for i in range(k + 2, TILE)}
            m = {i: (q[i][0] * inv, q[i][1] * inv) for i in q}
            for i in q:
                for c in range(k + 2, i + 1):
                    s[i][c] = s[i][c] - (q[i][0] * s[c][k] + q[i][1] * s[c][k + 1]) * inv
            r0, r1 = rows[k], rows[k + 1]
            v0, v1 = (d2 * r0 - d1 * r1) * inv, (d0 * r1 - d1 * r0) * inv
            steps.append((v0, v1, m))
            for i in q:
                rows[i] = rows[i] - (m[i][0] * r0 + m[i][1] * r1)
            for p in later[:1]:
                e0, e1 = e[p][k], e[p][k + 1]
                panel[p] = panel[p] - (e0 * v0 + e1 * v1)
                for i in q:
                    e[p][i] = e[p][i] - (m[i][0] * e0 + m[i][1] * e1)
            first = 1.0 / d0
            pivots = d0 if k == 0 else jnp.where(sub == k, d0, pivots)
            pivots = jnp.where(sub == k + 1, det * first, pivots)
            result = r0 if k == 0 else jnp.where(sub == k, r0, result)
            result = jnp.where(sub == k + 1, r1 - (d1 * first) * r0, result)
        out.append(jnp.where(lane < at + TILE, result * (lax.rsqrt(pivots) * root), 0.0))
        if t + 2 < n:
            v = [None] * TILE
            for k in reversed(range(0, TILE, 2)):
                v[k], v[k + 1], m = steps[k // 2]
                for i in m:
                    v[k] = v[k] - m[i][0] * v[i]
                    v[k + 1] = v[k + 1] - m[i][1] * v[i]
            for p in later[1:]:
                terms = [e[p][k] * v[k] for k in range(TILE)]
                while len(terms) > 1:
                    terms = [x + y for x, y in zip(terms[::2], terms[1::2])]
                panel[p] = panel[p] - terms[0]
    return out


def packing(rank, pair):
    at, out = 0, []
    for i in range(rank // pair - 1):
        size = rank - (i + 1) * pair
        out.append((i, at, size))
        at += size
    return out


def factor_kernel(near_hbm, far_hbm, packed_ref, inverse_ref, a, u_ref, near, far, held, sems):
    n_sh, n_chips, depth, width = near_hbm.shape
    rank = n_sh * depth
    near_copy = pltpu.make_async_copy(near_hbm, near, sems.at[0])
    far_copy = pltpu.make_async_copy(far_hbm, far, sems.at[1])
    near_copy.start()
    far_copy.start()
    a[...] = jnp.zeros_like(a)
    near_copy.wait()

    @pl.loop(0, n_chips)
    def _(i):
        add_gram(near[:, i].reshape(rank, width), a)

    far_copy.wait()

    @pl.loop(0, n_chips)
    def _(i):
        add_gram(far[:, i].reshape(rank, width), a)

    step, pair = LANES, 2 * LANES
    rc = ((1,), (0,))

    @pl.loop(0, rank // step)
    def _(j):
        r0 = pl.multiple_of(j * step, step)
        side = pl.multiple_of(lax.rem(j, 2) * step, step)
        for t, panel in enumerate(inverse_factor(a[pl.ds(r0, step), pl.ds(r0, step)], held)):
            inverse_ref[pl.ds(pl.multiple_of(r0 + TILE * t, TILE), TILE), pl.ds(side, step)] = panel
        inverse = inverse_ref[pl.ds(r0, step), pl.ds(side, step)]

        u_ref[pl.ds(r0, step), :] = dot(inverse, a[pl.ds(r0, step), :], rc)

        @pl.when(lax.rem(j, 2) == 0)
        def _():
            r1 = pl.multiple_of((j + 1) * step, step)
            ut = u_ref[pl.ds(r0, step), pl.ds(r1, step)].T
            inverse_ref[pl.ds(r0, step), step:] = jnp.zeros((step, step), f32)

            a[pl.ds(r1, step), :] -= dot(ut, u_ref[pl.ds(r0, step), :], rc)

        @pl.when(lax.rem(j, 2) == 1)
        def _():
            p0 = pl.multiple_of((j - 1) * step, pair)
            before = inverse_ref[pl.ds(p0, step), :step]
            cross = dot(u_ref[pl.ds(p0, step), pl.ds(r0, step)], before, ((0,), (0,)))
            inverse_ref[pl.ds(r0, step), :step] = -dot(inverse, cross, rc)

            @pl.loop((j + 1) // 2, rank // pair)
            def _(i):
                r1 = pl.multiple_of(i * pair, pair)
                ut = u_ref[pl.ds(p0, pair), pl.ds(r1, pair)].T

                @pl.loop(i, rank // pair)
                def _(c):
                    at = pl.multiple_of(c * pair, pair)
                    a[pl.ds(r1, pair), pl.ds(at, pair)] -= dot(ut, u_ref[pl.ds(p0, pair), pl.ds(at, pair)], rc)
    for i, at, size in packing(rank, pair):
        packed_ref[:, at : at + size] = u_ref[i * pair : (i + 1) * pair, rank - size :]


def factor(near, far):
    rank = near.shape[0] * near.shape[2]
    return pl.pallas_call(
        factor_kernel,
        out_shape=[
            jax.ShapeDtypeStruct((2 * LANES, sum(size for _, _, size in packing(rank, 2 * LANES))), f32),
            jax.ShapeDtypeStruct((rank, 2 * LANES), f32),
        ],
        in_specs=[pl.BlockSpec(memory_space=pl.ANY)] * 2,
        out_specs=[pl.BlockSpec(memory_space=pltpu.VMEM)] * 2,
        scratch_shapes=[
            pltpu.VMEM((rank, rank), f32),
            pltpu.VMEM((rank, rank), f32),
            pltpu.VMEM(near.shape, bf16),
            pltpu.VMEM(far.shape, bf16),
            pltpu.VMEM((TILE + 1, TILE, LANES), f32),
            pltpu.SemaphoreType.DMA((2,)),
        ],
        compiler_params=pltpu.CompilerParams(vmem_limit_bytes=28 * MIB),
        cost_estimate=pl.CostEstimate(flops=60_000_000_000, bytes_accessed=8 * rank * rank, transcendentals=0),
        name="factor",
    )(near, far)


def solve_kernel(scale, w_ref, u_ref, inverse_ref, x_ref, y, w):
    pair = 2 * LANES
    rank = w_ref.shape[1]
    n = rank // pair
    start = {i: at for i, at, _ in packing(rank, pair)}
    block = lambda j: slice(j * pair, (j + 1) * pair)
    for j in range(n):
        value = w_ref[:, block(j)]
        for i in range(j):
            at = start[i] + (j - i - 1) * pair
            value = value - dot(y[:, block(i)], u_ref[:, at : at + pair], ((1,), (0,)), HIGH)
        y[:, block(j)] = dot(value, inverse_ref[block(j), :], ((1,), (1,)), HIGH)
    for j in reversed(range(n)):
        value = y[:, block(j)]
        if j < n - 1:
            value = value - dot(
                w[:, (j + 1) * pair :], u_ref[:, start[j] : start[j] + rank - (j + 1) * pair], ((1,), (1,)), HIGH
            )
        x = dot(value, inverse_ref[block(j), :], ((1,), (0,)), HIGH)
        w[:, block(j)] = x
        x_ref[:, block(j)] = (x * scale).astype(bf16)


def solve(w, u, inverse, scale):
    return pl.pallas_call(
        functools.partial(solve_kernel, scale),
        out_shape=jax.ShapeDtypeStruct(w.shape, bf16),
        in_specs=[pl.BlockSpec(memory_space=pltpu.VMEM)] * 3,
        out_specs=pl.BlockSpec(memory_space=pltpu.VMEM),
        scratch_shapes=[pltpu.VMEM(w.shape, f32)] * 2,
        compiler_params=pltpu.CompilerParams(vmem_limit_bytes=16 * MIB),
        cost_estimate=pl.CostEstimate(flops=8_000_000_000, bytes_accessed=16 * 2**20, transcendentals=0),
        name="solve",
    )(w, u, inverse)


def shards(gradients, error_memory, q_factor):
    core = lax.axis_index(CORE)
    n_chips = lax.axis_size(CHIPS)
    n_dp = 2 * n_chips
    n_sh = lax.axis_size(SHARD)
    rows, cols = gradients.shape[1:]
    rank = q_factor.shape[1]
    own = -(-rows // (n_dp * LANES)) * LANES
    wide = -(-cols // (n_dp * 16)) * n_dp * 16
    gradient_t, error_t = gradients[0].T, error_memory[0].T

    with jax.named_scope("total"):
        mine, other = cut(core, gradient_t, error_t, n_chips, own)
        got = lax.ppermute(other, CORE, SWAP)
        pair = (mine.astype(f32) + got.astype(f32)).astype(bf16)
        arrived = lax.all_to_all(pair, CHIPS, 0, 0, tiled=True)
        total_t = jnp.sum(arrived.astype(f32), axis=0)

    with jax.named_scope("left"):
        part = dot(q_factor.astype(f32), total_t, ((0,), (0,)), HIGH).astype(bf16)
        arrived = lax.all_to_all(part.reshape(n_sh, rank // n_sh, own), SHARD, 0, 0, tiled=True)
        p_own = jnp.sum(arrived.astype(f32), axis=0).astype(bf16)
        p_near = spread(p_own, SHARD + CHIPS, n_sh * n_chips).reshape(n_sh, n_chips, rank // n_sh, own)
        p_far = lax.ppermute(p_near, CORE, SWAP)

    with jax.named_scope("right"):
        p_t = lax.dynamic_index_in_dim(p_near, lax.axis_index(CHIPS), 1, keepdims=False).reshape(rank, own)
        total_wide = jnp.pad(total_t, ((0, wide - cols), (0, 0)))
        w_part = dot(total_wide, p_t.astype(f32), ((1,), (1,)), HIGH)
        w_parts = lax.all_to_all(w_part.reshape(n_dp, wide // n_dp, rank), DP, 0, 0, tiled=True)

    with jax.named_scope("solve"):
        u, inverse = factor(p_near, p_far)
        w_parts, inverse = lax.optimization_barrier((w_parts, inverse))
        x_own = solve(jnp.sum(w_parts, axis=0), u, inverse, 1.0 / n_dp)

    with jax.named_scope("rebuild"):
        x_near = spread(x_own, CHIPS, n_chips)
        x_far = lax.ppermute(x_near, CORE, SWAP)
        rebuilt_t, new_error_t = finish(core, p_near, p_far, x_near, x_far, gradient_t, error_t)
    return (rebuilt_t.T, new_error_t.T[None])


def solution(mesh):
    fine = Mesh(mesh.devices.reshape(4, 2, 2, 2, 4), ("x", "yh", "c", "yl", "z"))
    in_specs = (P(DP, None, SHARD), P(DP, None, SHARD), P(SHARD, None))
    out_specs = (P(None, SHARD), P(DP, None, SHARD))
    return jax.shard_map(shards, mesh=fine, in_specs=in_specs, out_specs=out_specs, check_vma=False)
```
